256 devices in a mesh: grp: 4 (over y), tok: 32 (over z, x_lo, core), ch: 2 (over x_hi).
Axes of the slice: x: 4 (x_hi: 2, x_lo: 2; x = x_hi * 2 + x_lo), y: 4, z: 8, core: 2. Of those that a mesh axis runs over, the one named last changes fastest.
Arguments:
- tokens: bfloat16 [512, 512, 1024], P(('grp', 'tok'), None, 'ch'), may hold values from -6 to 6
- row_factor: bfloat16 [512, 512, 512], P(('grp', 'tok')), may hold values from -0.25 to 0.25
- column_factor: bfloat16 [512, 512, 512], P(('grp', 'tok')), may hold values from -0.25 to 0.25
- kernel: bfloat16 [3, 3, 1024], P(None, None, 'ch'), may hold values from -2 to 2
- cotangent: bfloat16 [512, 512, 1024], P(('grp', 'tok'), None, 'ch'), may hold values from -6 to 6
Outputs:
- grad_tokens: bfloat16 [512, 512, 1024], P(('grp', 'tok'), None, 'ch')
- grad_row: bfloat16 [512, 512, 512], P(('grp', 'tok'), 'ch')
- grad_column: bfloat16 [512, 512, 512], P(('grp', 'tok'), 'ch')
- grad_kernel: float32 [3, 3, 1024], P(None, None, 'ch')
The draws below stay inside these ranges and needn't reach their ends.
All inputs are finite; a program needn't handle non-finite values.
Results may differ from the reference program's by a relative error of at most 0.0058.
Values may be sent and summed in bfloat16 or wider, within the bound.
A program may use at most 128 MiB of HBM per device.

```python
import jax
import jax.numpy as jnp

NR = 512
NC = 512
D = 1024


def levels(rng, shape, split, least, top_value):
    def one(position, parts):
        heights = jax.random.uniform(jax.random.fold_in(jax.random.fold_in(rng, 6), position), (parts,), jnp.float32, least / len(split), top_value / len(split))
        return jnp.repeat(jnp.exp(heights), shape[position] // parts).reshape((-1,) + (1,) * (len(shape) - position - 1))

    level = one(*split[0])
    for cut in split[1:]:
        level = level * one(*cut)
    return level


def scatter_about(rng, shape, spread, most, cuts=(), kind=jnp.bfloat16):
    factor_of = levels(rng, shape, cuts, -0.22, 0.18) if cuts else 1.0
    values = jax.random.normal(rng, shape, jnp.float32) * spread * factor_of
    return jnp.minimum(jnp.maximum(values, -most), most).astype(kind)


def setup_inputs(seed: int = 0) -> dict:
    arg_keys = jax.random.split(jax.random.key(seed), 6)
    return {
        "tokens": scatter_about(arg_keys[0], (NR, NC, D), 1.0, 6.0, ((0, 128), (2, 2))),
        "row_factor": scatter_about(arg_keys[1], (NR, NC, NC), NC ** -0.5, 0.25, ((0, 128),)),
        "column_factor": scatter_about(arg_keys[2], (NC, NR, NR), NR ** -0.5, 0.25, ((0, 128),)),
        "kernel": scatter_about(arg_keys[3], (3, 3, D), 9 ** -0.5, 2.0, ((2, 2),)),
        "cotangent": scatter_about(arg_keys[4], (NR, NC, D), 1.0, 6.0, ((0, 128), (2, 2))),
    }


def reference(tokens, row_factor, column_factor, kernel, cotangent):
    tok_f = tokens.astype(jnp.float32)
    row_f = row_factor.astype(jnp.float32)
    col_f = column_factor.astype(jnp.float32)
    mixed_rows = jnp.einsum('rce,red->rcd', row_f, tok_f).astype(jnp.bfloat16)
    mixed = jnp.einsum('crs,scd->rcd', col_f, mixed_rows.astype(jnp.float32)).astype(jnp.bfloat16)
    gate = jax.nn.sigmoid(tok_f)
    mixed_f = mixed.astype(jnp.float32)
    gated = (mixed_f * gate).astype(jnp.bfloat16)
    cot_f = cotangent.astype(jnp.float32)
    cot_pad = jnp.pad(cot_f, ((1, 1), (1, 1), (0, 0)))
    gated_pad = jnp.pad(gated.astype(jnp.float32), ((1, 1), (1, 1), (0, 0)))
    kern_f = kernel.astype(jnp.float32)
    grad_gated = jnp.zeros_like(tok_f)
    kernel_rows = []
    for i in range(3):
        kernel_cols = []
        for j in range(3):
            grad_gated = grad_gated + kern_f[i, j] * cot_pad[2 - i:2 - i + NR, 2 - j:2 - j + NC]
            kernel_cols.append(jnp.sum(gated_pad[i:i + NR, j:j + NC] * cot_f, axis=(0, 1)))
        kernel_rows.append(jnp.stack(kernel_cols))
    grad_kernel = jnp.stack(kernel_rows)
    grad_mixed = (grad_gated * gate).astype(jnp.bfloat16)
    grad_gate_in = grad_gated * mixed_f * gate * (1.0 - gate)
    grad_mixed_f = grad_mixed.astype(jnp.float32)
    grad_rows = jnp.einsum('crs,rcd->scd', col_f, grad_mixed_f).astype(jnp.bfloat16)
    grad_column = jnp.einsum('rcd,scd->crs', grad_mixed_f, mixed_rows.astype(jnp.float32)).astype(jnp.bfloat16)
    grad_rows_f = grad_rows.astype(jnp.float32)
    grad_row = jnp.einsum('rcd,red->rce', grad_rows_f, tok_f).astype(jnp.bfloat16)
    grad_tokens = (jnp.einsum('rce,rcd->red', row_f, grad_rows_f) + grad_gate_in).astype(jnp.bfloat16)
    return grad_tokens, grad_row, grad_column, grad_kernel
```

```python
import functools

import jax
import jax.numpy as jnp
from jax import lax
from jax.experimental import pallas as pl
from jax.experimental.pallas import tpu as pltpu
from jax.sharding import PartitionSpec as P

MESH = pl.DeviceIdType.MESH
GRP, TOK = 4, 32
N = GRP * TOK


def place():
    return lax.axis_index("grp") * TOK + lax.axis_index("tok")


def device(t):
    return (t // TOK, lax.rem(t, TOK), lax.axis_index("ch"))


def exchange_kernel(count, *refs):
    srcs, dsts, (send_sem, recv_sem) = refs[:count], refs[count : 2 * count], refs[2 * count :]
    me = place()
    barrier = pltpu.get_barrier_semaphore()

    def greet(i, carry):
        t = lax.rem(me + i, N)
        pl.semaphore_signal(barrier, inc=1, device_id=device(t), device_id_type=MESH)
        return carry

    lax.fori_loop(1, N, greet, 0)
    pl.semaphore_wait(barrier, N - 1)
    for k in range(count):
        pltpu.make_async_copy(srcs[k].at[me], dsts[k].at[me], recv_sem.at[k]).start()

        def send(i, carry):
            t = lax.rem(me + i, N)
            pltpu.make_async_remote_copy(
                src_ref=srcs[k].at[t],
                dst_ref=dsts[k].at[me],
                send_sem=send_sem.at[k],
                recv_sem=recv_sem.at[k],
                device_id=device(t),
                device_id_type=MESH,
            ).start()
            return carry

        lax.fori_loop(1, N, send, 0)
    for k in range(count):
        pltpu.make_async_copy(
            srcs[k].at[pl.ds(0, N - 1)], dsts[k].at[pl.ds(0, N - 1)], send_sem.at[k]
        ).wait()
        pltpu.make_async_copy(srcs[k], dsts[k], recv_sem.at[k]).wait()


def exchange(call_id, *arrays):
    count = len(arrays)
    spec = pl.BlockSpec(memory_space=pltpu.VMEM)
    return pl.pallas_call(
        functools.partial(exchange_kernel, count),
        out_shape=[jax.ShapeDtypeStruct(a.shape, a.dtype) for a in arrays],
        in_specs=[spec] * count,
        out_specs=[spec] * count,
        scratch_shapes=[pltpu.SemaphoreType.DMA((count,)), pltpu.SemaphoreType.DMA((count,))],
        name="exchange",
        compiler_params=pltpu.CompilerParams(
            collective_id=call_id, has_side_effects=True, vmem_limit_bytes=24 * 2**20
        ),
    )(*arrays)


def sum_kernel(x_ref, o_ref, held, send_sem, recv_sem):
    y, tok, h = lax.axis_index("grp"), lax.axis_index("tok"), lax.axis_index("ch")
    z, xc = tok // 4, lax.rem(tok, 4)
    steps = (
        (8, lambda i: (y, lax.rem(z + i, 8) * 4 + xc, h)),
        (4, lambda i: (lax.rem(y + i, 4), tok, h)),
        (4, lambda i: (y, z * 4 + lax.rem(xc + i, 4), h)),
    )
    barrier = pltpu.get_barrier_semaphore()
    for size, peer in steps:
        for i in range(1, size):
            pl.semaphore_signal(barrier, inc=1, device_id=peer(i), device_id_type=MESH)
    pl.semaphore_wait(barrier, 13)
    o_ref[...] = x_ref[...]
    slot = 0
    for k, (size, peer) in enumerate(steps):
        for i in range(1, size):
            pltpu.make_async_remote_copy(
                src_ref=o_ref,
                dst_ref=held.at[slot + i - 1],
                send_sem=send_sem.at[k],
                recv_sem=recv_sem.at[k],
                device_id=peer(i),
                device_id_type=MESH,
            ).start()
        span = held.at[pl.ds(slot, size - 1)]
        pltpu.make_async_copy(span, span, send_sem.at[k]).wait()
        pltpu.make_async_copy(span, span, recv_sem.at[k]).wait()
        o_ref[...] = o_ref[...] + jnp.sum(held[slot : slot + size - 1], axis=0)
        slot += size - 1


def sum_cells(x):
    spec = pl.BlockSpec(memory_space=pltpu.VMEM)
    return pl.pallas_call(
        sum_kernel,
        out_shape=jax.ShapeDtypeStruct(x.shape, x.dtype),
        in_specs=[spec],
        out_specs=spec,
        scratch_shapes=[
            pltpu.VMEM((13,) + x.shape, x.dtype),
            pltpu.SemaphoreType.DMA((3,)),
            pltpu.SemaphoreType.DMA((3,)),
        ],
        name="sum_cells",
        compiler_params=pltpu.CompilerParams(collective_id=7, has_side_effects=True),
    )(x)


def rim(cells):
    perm = [(i, i + 1) for i in range(N - 1)]
    back = [(i + 1, i) for i in range(N - 1)]
    return jnp.concatenate(
        [
            lax.ppermute(cells[-1:], ("grp", "tok"), perm),
            cells,
            lax.ppermute(cells[:1], ("grp", "tok"), back),
        ],
        axis=0,
    )


def pack(local):
    rows, cols, chans = local.shape
    return local.reshape(rows, N, cols // N, chans).transpose(1, 0, 2, 3).reshape(N, -1, chans)


def shards(tokens, row_factor, column_factor, kernel, cotangent):
    rows, cols, chans = tokens.shape
    wide = cols // N
    mixed_rows = jnp.einsum(
        "rce,red->rcd", row_factor, tokens, preferred_element_type=jnp.float32
    ).astype(jnp.bfloat16)
    gate = jax.nn.sigmoid(tokens.astype(jnp.float32))
    cot_pad = jnp.pad(rim(cotangent), ((0, 0), (1, 1), (0, 0))).astype(jnp.float32)
    kern_f = kernel.astype(jnp.float32)
    grad_gated = jnp.zeros((rows, cols, chans), jnp.float32)
    for i in range(3):
        for j in range(3):
            grad_gated = (
                grad_gated + kern_f[i, j] * cot_pad[2 - i : 2 - i + rows, 2 - j : 2 - j + cols]
            )
    grad_mixed = (grad_gated * gate).astype(jnp.bfloat16)
    got_mixed, got_grad = exchange(1, pack(mixed_rows), pack(grad_mixed))

    def columns(got):
        return got.reshape(N, rows, wide, chans).transpose(2, 0, 1, 3).reshape(wide, N * rows, chans)

    col_mixed, col_grad = columns(got_mixed), columns(got_grad)
    mixed_cols = jnp.einsum(
        "crs,csd->crd", column_factor, col_mixed, preferred_element_type=jnp.float32
    ).astype(jnp.bfloat16)
    grad_cols = jnp.einsum(
        "crs,crd->csd", column_factor, col_grad, preferred_element_type=jnp.float32
    ).astype(jnp.bfloat16)
    column_terms = jnp.einsum(
        "crd,csd->crs", col_grad, col_mixed, preferred_element_type=jnp.float32
    )
    grad_column = lax.psum_scatter(column_terms, "ch", scatter_dimension=1, tiled=True).astype(
        jnp.bfloat16
    )

    def unpack_columns(local):
        return (
            local.reshape(wide, N, rows, chans).transpose(1, 2, 0, 3).reshape(N, rows * wide, chans)
        )

    back_mixed, back_grad = exchange(2, unpack_columns(mixed_cols), unpack_columns(grad_cols))

    def by_rows(got):
        return got.reshape(N, rows, wide, chans).transpose(1, 0, 2, 3).reshape(rows, cols, chans)

    mixed, grad_rows = by_rows(back_mixed), by_rows(back_grad)
    mixed_f = mixed.astype(jnp.float32)
    gated = (mixed_f * gate).astype(jnp.bfloat16).astype(jnp.float32)
    kernel_rows = []
    for i in range(3):
        for j in range(3):
            kernel_rows.append(
                jnp.sum(gated * cot_pad[2 - i : 2 - i + rows, 2 - j : 2 - j + cols], axis=(0, 1))
            )
    grad_kernel = sum_cells(jnp.pad(jnp.stack(kernel_rows), ((0, 7), (0, 0))))
    grad_kernel = grad_kernel[:9].reshape(3, 3, chans)
    grad_gate_in = grad_gated * mixed_f * gate * (1.0 - gate)
    row_terms = jnp.einsum("rcd,red->rce", grad_rows, tokens, preferred_element_type=jnp.float32)
    grad_row = lax.psum_scatter(row_terms, "ch", scatter_dimension=1, tiled=True).astype(
        jnp.bfloat16
    )
    back = jnp.einsum("rce,rcd->red", row_factor, grad_rows, preferred_element_type=jnp.float32)
    grad_tokens = (back + grad_gate_in).astype(jnp.bfloat16)
    return (grad_tokens, grad_row, grad_column, grad_kernel)


def solution(mesh):
    return jax.shard_map(
        shards,
        mesh=mesh,
        in_specs=(
            P(("grp", "tok"), None, "ch"),
            P(("grp", "tok"), None, None),
            P(("grp", "tok"), None, None),
            P(None, None, "ch"),
            P(("grp", "tok"), None, "ch"),
        ),
        out_specs=(
            P(("grp", "tok"), None, "ch"),
            P(("grp", "tok"), "ch", None),
            P(("grp", "tok"), "ch", None),
            P(None, None, "ch"),
        ),
        check_vma=False,
    )
```

```python
import jax
import jax.numpy as jnp
from jax import lax
from jax.experimental import pallas as pl
from jax.experimental.pallas import tpu as pltpu
from jax.sharding import PartitionSpec as P

MESH = pl.DeviceIdType.MESH
F32, BF16 = jnp.float32, jnp.bfloat16
Y, Z, XC = 4, 8, 4
N = Y * Z * XC
ROWS = 4
SIZE = 512
CELL = ROWS * ROWS
BAND = SIZE // Y
EDGE = 16
STEP = 128


def dot(a, b, contract=((1,), (0,))):
    return lax.dot_general(a, b, (contract, ((), ())), preferred_element_type=F32)


def aligned(value, multiple):
    return pl.multiple_of(value, multiple)


def mixer(
    tok_h, rf_h, cf_h, kern, cot_h,
    gtok_h, grow_h, gcol_h, gkern,
    tok, rf, cf, cotp, s1, s2, r1, r2, r3, r4, xs, gs, hold, mid, grows,
    row_out, col_out, row_got, col_got, row_done, col_done, taps, kf, total, held, t1, t2,
    load_sem, halo_send, halo_recv, send_sem, recv_sem, last_sem,
    col_send, col_recv, row_send, row_recv, sum_send, sum_recv, store_sem,
):
    y, tk, h = lax.axis_index("grp"), lax.axis_index("tok"), lax.axis_index("ch")
    z, xc = tk // XC, lax.rem(tk, XC)
    me = y * (Z * XC) + tk
    other = (y, tk, 1 - h)

    def device(t):
        return (t // (Z * XC), lax.rem(t, Z * XC), h)

    loads = [
        pltpu.make_async_copy(tok_h, tok, load_sem.at[0]),
        pltpu.make_async_copy(rf_h, rf, load_sem.at[1]),
        pltpu.make_async_copy(cot_h, cotp.at[pl.ds(1, ROWS), pl.ds(EDGE, SIZE), :], load_sem.at[2]),
        pltpu.make_async_copy(cf_h, cf, load_sem.at[3]),
    ]
    for load in loads:
        load.start()

    barrier = pltpu.get_barrier_semaphore()

    def greet(i, carry):
        pl.semaphore_signal(
            barrier, inc=1, device_id=device(lax.rem(me + i, N)), device_id_type=MESH
        )
        return carry

    lax.fori_loop(1, N, greet, 0)
    pl.semaphore_signal(barrier, inc=1, device_id=other, device_id_type=MESH)

    out = lax.broadcasted_iota(jnp.int32, (256, 256), 0)
    src = lax.broadcasted_iota(jnp.int32, (256, 256), 1)
    first, second, third = out >> 4, (out >> 2) & 3, out & 3
    t1[...] = (src == second * 64 + first * 4 + third).astype(F32).astype(BF16)
    first, second, third = out >> 6, (out >> 2) & 15, out & 3
    t2[...] = (src == second * 16 + third * 4 + first).astype(F32).astype(BF16)
    cotp[:, 0:EDGE, :] = jnp.zeros((ROWS + 2, EDGE, SIZE), BF16)
    cotp[:, EDGE + SIZE :, :] = jnp.zeros((ROWS + 2, EDGE, SIZE), BF16)
    for i in range(3):
        kf[3 * i : 3 * i + 3, :] = kern[i].astype(F32)
    taps[...] = jnp.zeros_like(taps)

    up, down = lax.rem(me + N - 1, N), lax.rem(me + 1, N)
    halos = [
        pltpu.make_async_remote_copy(
            src_ref=cot_h.at[ROWS - 1],
            dst_ref=cotp.at[0, pl.ds(EDGE, SIZE), :],
            send_sem=halo_send.at[0],
            recv_sem=halo_recv.at[0],
            device_id=device(down),
            device_id_type=MESH,
        ),
        pltpu.make_async_remote_copy(
            src_ref=cot_h.at[0],
            dst_ref=cotp.at[ROWS + 1, pl.ds(EDGE, SIZE), :],
            send_sem=halo_send.at[1],
            recv_sem=halo_recv.at[1],
            device_id=device(up),
            device_id_type=MESH,
        ),
    ]

    def pack(band, parts, buf):
        for half in range(2):
            stack = jnp.concatenate([p[64 * half : 64 * half + 64] for p in parts], axis=0)
            at = aligned(band * (Z * XC * CELL) + half * 256, 256)
            buf[pl.ds(at, 256), :] = dot(t1[...], stack).astype(BF16)

    def send(dy, buf, dst, k, sems):
        band = lax.rem(y + dy, Y)
        mine = aligned(me * CELL, CELL)

        @pl.when(dy == 0)
        def _():
            pltpu.make_async_copy(
                buf.at[pl.ds(mine, CELL), :], dst.at[pl.ds(mine, CELL), :], sems(0)
            ).start()

        def one(i, carry):
            par = i // 16
            dz = lax.rem(i // 4, 4) * 2 + par
            t = band * (Z * XC) + lax.rem(z + dz, Z) * XC + lax.rem(xc + i, XC)
            pltpu.make_async_remote_copy(
                src_ref=buf.at[pl.ds(aligned(t * CELL, CELL), CELL), :],
                dst_ref=dst.at[pl.ds(mine, CELL), :],
                send_sem=send_sem.at[k],
                recv_sem=sems(dy * 2 + par),
                device_id=device(t),
                device_id_type=MESH,
            ).start()
            return carry

        lax.fori_loop(jnp.where(dy == 0, 1, 0), Z * XC, one, 0)

    def wait_sent(buf, k):
        part = buf.at[pl.ds(0, (N - 1) * CELL), :]
        pltpu.make_async_copy(part, part, send_sem.at[k]).wait()

    def wait_got(buf, k):
        pltpu.make_async_copy(buf, buf, recv_sem.at[k]).wait()

    def unpack(buf, dst):
        def one(b, carry):
            block = dot(t2[...], buf[pl.ds(aligned(b * 256, 256), 256), :]).astype(BF16)
            for w in range(ROWS):
                dst[w, pl.ds(aligned(b * 64, 64), 64), :] = block[64 * w : 64 * w + 64]
            return carry

        lax.fori_loop(0, N * CELL // 256, one, 0)

    def band_of(dy):
        band = lax.rem(y + dy, Y)
        return band, pl.ds(aligned(band * BAND, BAND), BAND)

    loads[0].wait()
    loads[1].wait()

    def mix_rows(dy, carry):
        band, cols = band_of(dy)
        pack(band, [dot(rf[q, cols, :], tok[q]).astype(BF16) for q in range(ROWS)], s1)

        @pl.when(dy == 0)
        def _():
            pl.semaphore_wait(barrier, N)
            for halo in halos:
                halo.start()

        send(dy, s1, r1, 0, lambda g: recv_sem.at[0])
        return carry

    lax.fori_loop(0, Y, mix_rows, 0)

    loads[2].wait()
    for halo in halos:
        halo.wait_recv()

    @pl.when(me == 0)
    def _():
        cotp[0, EDGE : EDGE + SIZE, :] = jnp.zeros((SIZE, SIZE), BF16)

    @pl.when(me == N - 1)
    def _():
        cotp[ROWS + 1, EDGE : EDGE + SIZE, :] = jnp.zeros((SIZE, SIZE), BF16)

    parts = SIZE // STEP

    def tile(it):
        r = it // (parts * parts)
        at = aligned(lax.rem(it // parts, parts) * STEP, STEP)
        lanes = pl.ds(aligned(lax.rem(it, parts) * STEP, STEP), STEP)
        wide = pl.ds(at, STEP + 2 * EDGE)
        return r, pl.ds(at, STEP), wide, lanes

    inner = slice(EDGE, EDGE + STEP)
    span = STEP + 2 * EDGE

    def shifted(x):
        return (pltpu.roll(x, span - 1, 0)[inner], x[inner], pltpu.roll(x, 1, 0)[inner])

    def conv(it, carry):
        r, cols, wide, lanes = tile(it)
        rows = [cotp[r + 2 - i, wide, lanes].astype(F32) for i in range(3)]
        sums = []
        for j in range(3):
            term = rows[0] * kf[j : j + 1, lanes]
            for i in (1, 2):
                term = term + rows[i] * kf[3 * i + j : 3 * i + j + 1, lanes]
            sums.append(term)
        grad = (
            pltpu.roll(sums[0], span - 1, 0)[inner]
            + sums[1][inner]
            + pltpu.roll(sums[2], 1, 0)[inner]
        )
        gate = jax.nn.sigmoid(tok[r, cols, lanes].astype(F32))
        grad = grad * gate
        mid[r, cols, lanes] = grad.astype(BF16)
        hold[r, cols, lanes] = grad * (1.0 - gate)
        return carry

    lax.fori_loop(0, ROWS * parts * parts, conv, 0)

    def send_grad(dy, carry):
        band, cols = band_of(dy)
        pack(band, [mid[q, cols, :] for q in range(ROWS)], s2)
        send(dy, s2, r2, 1, lambda g: recv_sem.at[1])
        return carry

    lax.fori_loop(0, Y, send_grad, 0)

    loads[3].wait()
    wait_got(r1, 0)
    unpack(r1, xs)
    wait_sent(s1, 0)

    def mix_columns(dy, carry):
        band, cols = band_of(dy)
        pack(band, [dot(cf[q, cols, :], xs[q]).astype(BF16) for q in range(ROWS)], s1)
        send(dy, s1, r3, 2, lambda g: recv_sem.at[2])
        return carry

    lax.fori_loop(0, Y, mix_columns, 0)

    wait_got(r2, 1)
    unpack(r2, gs)
    wait_sent(s2, 1)

    def back_columns(dy, carry):
        band, cols = band_of(dy)
        pack(
            band,
            [dot(cf[q, :, cols], gs[q], ((0,), (0,))).astype(BF16) for q in range(ROWS)],
            s2,
        )
        send(dy, s2, r4, 3, lambda g: last_sem.at[g])
        return carry

    lax.fori_loop(0, Y, back_columns, 0)

    def half_of(which):
        return pl.ds(aligned(which * (SIZE // 2), SIZE // 2), SIZE // 2)

    def column_copy(q):
        return pltpu.make_async_remote_copy(
            src_ref=col_out.at[q],
            dst_ref=col_got.at[q],
            send_sem=col_send.at[q],
            recv_sem=col_recv.at[q],
            device_id=other,
            device_id_type=MESH,
        )

    def column_away(q, carry):
        col_out[q] = dot(gs[q, half_of(1 - h), :], xs[q], ((1,), (1,))).astype(BF16)
        column_copy(q).start()
        return carry

    lax.fori_loop(0, ROWS, column_away, 0)

    wait_got(r3, 2)
    unpack(r3, mid)

    def gated(it, carry):
        r, cols, wide, lanes = tile(it)
        mixed = mid[r, cols, lanes].astype(F32)
        gate = jax.nn.sigmoid(tok[r, cols, lanes].astype(F32))
        cells = (mixed * gate).astype(BF16).astype(F32)
        hold[r, cols, lanes] = hold[r, cols, lanes] * mixed
        for i in range(3):
            row = cotp[r + 2 - i, wide, lanes].astype(F32)
            for j, moved in enumerate(shifted(row)):
                term = (cells * moved).reshape(STEP // 8, 8, STEP)
                taps[3 * i + j, :, lanes] += jnp.sum(term, axis=0)
        return carry

    lax.fori_loop(0, ROWS * parts * parts, gated, 0)

    steps = (
        (Z, 0, lambda i: (y, lax.rem(z + i, Z) * XC + xc, h)),
        (Y, Z - 1, lambda i: (lax.rem(y + i, Y), tk, h)),
        (XC, Z + Y - 2, lambda i: (y, z * XC + lax.rem(xc + i, XC), h)),
    )

    def sum_start(k):
        size, slot, peer = steps[k]
        for i in range(1, size):
            pltpu.make_async_remote_copy(
                src_ref=total.at[k],
                dst_ref=held.at[slot + i - 1],
                send_sem=sum_send.at[k],
                recv_sem=sum_recv.at[k],
                device_id=peer(i),
                device_id_type=MESH,
            ).start()

    def sum_finish(k):
        size, slot, _ = steps[k]
        part = held.at[pl.ds(slot, size - 1)]
        pltpu.make_async_copy(part, part, sum_recv.at[k]).wait()
        total[k + 1] = total[k] + jnp.sum(held[slot : slot + size - 1], axis=0)

    def sum_sent(k):
        size, slot, _ = steps[k]
        part = held.at[pl.ds(slot, size - 1)]
        pltpu.make_async_copy(part, part, sum_send.at[k]).wait()

    total[0] = jnp.zeros((16, SIZE), F32)
    for k in range(9):
        total[0, k : k + 1, :] = jnp.sum(taps[k], axis=0, keepdims=True)
    sum_start(0)

    def column_store(q):
        return pltpu.make_async_copy(col_done.at[q], gcol_h.at[q], store_sem.at[q])

    def column_here(q, carry):
        term = dot(gs[q, half_of(h), :], xs[q], ((1,), (1,)))
        column_copy(q).wait_recv()
        col_done[q] = (term + col_got[q].astype(F32)).astype(BF16)
        column_store(q).start()
        return carry

    lax.fori_loop(0, ROWS, column_here, 0)
    sum_finish(0)
    sum_start(1)

    def source(dy):
        band = lax.rem(y + Y - dy, Y)
        return band, band // 2 != h, aligned(lax.rem(band, 2) * BAND, BAND)

    def row_copy(at):
        part = pl.ds(at, 16)
        return pltpu.make_async_remote_copy(
            src_ref=row_out.at[:, part, :],
            dst_ref=row_got.at[:, part, :],
            send_sem=row_send.at[at // BAND],
            recv_sem=row_recv.at[at // BAND],
            device_id=other,
            device_id_type=MESH,
        )

    def row_store(slot):
        part = pl.ds(slot * BAND, BAND)
        return pltpu.make_async_copy(
            row_done.at[:, part, :], grow_h.at[:, part, :], store_sem.at[ROWS + slot]
        )

    def row_here(dy):
        band, away, base = source(dy)

        @pl.when(jnp.logical_not(away))
        def _():
            part = pl.ds(base, BAND)
            got = row_got.at[:, part, :]
            pltpu.make_async_copy(got, got, row_recv.at[base // BAND]).wait()
            cols = pl.ds(aligned(band * BAND, BAND), BAND)
            for q in range(ROWS):
                term = dot(grows[q, cols, :], tok[q], ((1,), (1,)))
                row_done[q, part, :] = (term + row_got[q, part, :].astype(F32)).astype(BF16)
            row_store(base // BAND).start()

    def arrive(dy, carry):
        band, away, base = source(dy)
        for par in range(2):
            g = dy * 2 + par
            part = r4.at[pl.ds(0, 256), :]
            pltpu.make_async_copy(part, part, last_sem.at[g]).wait()
            zp = lax.rem(z + par, 2)
            blocks = [
                r4[pl.ds(aligned((band * Z + zp + 2 * m) * 64, 64), 64), :] for m in range(4)
            ]
            block = dot(t2[...], jnp.concatenate(blocks, axis=0)).astype(BF16)
            for q in range(ROWS):
                for m in range(4):
                    at = aligned(band * BAND + (zp + 2 * m) * 16, 16)
                    low = 64 * q + 16 * m
                    grows[q, pl.ds(at, 16), :] = block[low : low + 16]

            @pl.when(away)
            def _():
                for q in range(ROWS):
                    term = dot(block[64 * q : 64 * q + 64], tok[q], ((1,), (1,))).astype(BF16)
                    for m in range(4):
                        at = aligned(base + (zp + 2 * m) * 16, 16)
                        row_out[q, pl.ds(at, 16), :] = term[16 * m : 16 * m + 16]
                for m in range(4):
                    row_copy(aligned(base + (zp + 2 * m) * 16, 16)).start()

        cols = pl.ds(aligned(band * BAND, BAND), BAND)
        for q in range(ROWS):
            hold[q] = hold[q] + dot(rf[q, cols, :], grows[q, cols, :], ((0,), (0,)))

        @pl.when(dy > 0)
        def _():
            row_here(dy - 1)

        @pl.when(dy == 0)
        def _():
            sum_finish(1)
            sum_start(2)

        return carry

    lax.fori_loop(0, Y, arrive, 0)

    def token_store(q):
        return pltpu.make_async_copy(mid.at[q], gtok_h.at[q], store_sem.at[ROWS + 2 + q])

    def token_out(q, carry):
        mid[q] = hold[q].astype(BF16)
        token_store(q).start()
        return carry

    lax.fori_loop(0, ROWS, token_out, 0)
    sum_finish(2)
    for i in range(3):
        gkern[i] = total[3, 3 * i : 3 * i + 3, :]
    row_here(Y - 1)

    wait_sent(s1, 2)
    wait_sent(s2, 3)
    for halo in halos:
        halo.wait_send()
    for k in range(3):
        sum_sent(k)
    for slot in range(2):
        part = row_out.at[:, pl.ds(slot * BAND, BAND), :]
        pltpu.make_async_copy(part, part, row_send.at[slot]).wait()
        row_store(slot).wait()
    for q in range(ROWS):
        column_copy(q).wait_send()
        column_store(q).wait()
        token_store(q).wait()


def shards(tokens, row_factor, column_factor, kernel, cotangent):
    full = (ROWS, SIZE, SIZE)
    half = (ROWS, SIZE // 2, SIZE)
    flat = (N * CELL, SIZE)
    vmem, dma = pltpu.VMEM, pltpu.SemaphoreType.DMA
    whole = pl.BlockSpec(memory_space=pl.ANY)
    local = pl.BlockSpec(memory_space=pltpu.VMEM)
    return pl.pallas_call(
        mixer,
        out_shape=[
            jax.ShapeDtypeStruct(full, BF16),
            jax.ShapeDtypeStruct(half, BF16),
            jax.ShapeDtypeStruct(half, BF16),
            jax.ShapeDtypeStruct((3, 3, SIZE), F32),
        ],
        in_specs=[whole, whole, whole, local, whole],
        out_specs=[whole, whole, whole, local],
        scratch_shapes=[
            vmem(full, BF16), vmem(full, BF16), vmem(full, BF16),
            vmem((ROWS + 2, SIZE + 2 * EDGE, SIZE), BF16),
            vmem(flat, BF16), vmem(flat, BF16),
            vmem(flat, BF16), vmem(flat, BF16), vmem(flat, BF16), vmem(flat, BF16),
            vmem(full, BF16), vmem(full, BF16), vmem(full, F32), vmem(full, BF16), vmem(full, BF16),
            vmem(half, BF16), vmem(half, BF16), vmem(half, BF16), vmem(half, BF16),
            vmem(half, BF16), vmem(half, BF16),
            vmem((9, 8, SIZE), F32), vmem((16, SIZE), F32),
            vmem((4, 16, SIZE), F32), vmem((Z + Y + XC - 3, 16, SIZE), F32),
            vmem((256, 256), BF16), vmem((256, 256), BF16),
            dma((4,)), dma((2,)), dma((2,)), dma((4,)), dma((3,)), dma((2 * Y,)),
            dma((ROWS,)), dma((ROWS,)), dma((2,)), dma((2,)), dma((3,)), dma((3,)),
            dma((2 * ROWS + 2,)),
        ],
        name="mixer",
        compiler_params=pltpu.CompilerParams(
            collective_id=1, has_side_effects=True, vmem_limit_bytes=58 * 2**20
        ),
        cost_estimate=pl.CostEstimate(
            flops=7 * 10**9, bytes_accessed=12 * 2**20, transcendentals=4 * 10**6
        ),
    )(tokens, row_factor, column_factor, kernel, cotangent)


def solution(mesh):
    return jax.shard_map(
        lambda *args: tuple(shards(*args)),
        mesh=mesh,
        in_specs=(
            P(("grp", "tok"), None, "ch"),
            P(("grp", "tok"), None, None),
            P(("grp", "tok"), None, None),
            P(None, None, "ch"),
            P(("grp", "tok"), None, "ch"),
        ),
        out_specs=(
            P(("grp", "tok"), None, "ch"),
            P(("grp", "tok"), "ch", None),
            P(("grp", "tok"), "ch", None),
            P(None, None, "ch"),
        ),
        check_vma=False,
    )
```

```python
import jax
import jax.numpy as jnp
from jax import lax
from jax.experimental import pallas as pl
from jax.experimental.pallas import tpu as pltpu
from jax.sharding import PartitionSpec as P

MESH = pl.DeviceIdType.MESH
F32, BF16 = jnp.float32, jnp.bfloat16
Y, Z, XC = 4, 8, 4
N = Y * Z * XC
ROWS = 4
SIZE = 512
CELL = ROWS * ROWS
BAND = SIZE // Y
EDGE = 16
STEP = 128


def dot(a, b, contract=((1,), (0,))):
    return lax.dot_general(a, b, (contract, ((), ())), preferred_element_type=F32)


def aligned(value, multiple):
    return pl.multiple_of(value, multiple)


def mixer(
    tok_h, rf_h, cf_h, kern, cot_h,
    gtok_h, grow_h, gcol_h, gkern,
    tok, rf, cf, cotp, s1, s2, r1, r2, r3, r4, xs, gs, hold, mid, grows,
    row_out, col_out, row_got, col_got, row_done, col_done, relay, taps, kf, total, held, t1, t2,
    load_sem, halo_send, halo_recv, hand_send, hand_recv, pass_send, send_sem, recv_sem, last_sem,
    col_send, col_recv, row_send, row_recv, sum_send, sum_recv, store_sem,
):
    y, tk, h = lax.axis_index("grp"), lax.axis_index("tok"), lax.axis_index("ch")
    z, xc = tk // XC, lax.rem(tk, XC)
    me = y * (Z * XC) + tk
    other = (y, tk, 1 - h)

    def device(t):
        return (t // (Z * XC), lax.rem(t, Z * XC), h)

    loads = [
        pltpu.make_async_copy(tok_h, tok, load_sem.at[0]),
        pltpu.make_async_copy(rf_h, rf, load_sem.at[1]),
        pltpu.make_async_copy(cot_h, cotp.at[pl.ds(1, ROWS), pl.ds(EDGE, SIZE), :], load_sem.at[2]),
        pltpu.make_async_copy(cf_h, cf, load_sem.at[3]),
    ]
    for load in loads[:2]:
        load.start()

    barrier = pltpu.get_barrier_semaphore()

    def greet(i, carry):
        pl.semaphore_signal(
            barrier, inc=1, device_id=device(lax.rem(me + i, N)), device_id_type=MESH
        )
        return carry

    lax.fori_loop(1, N, greet, 0)
    pl.semaphore_signal(barrier, inc=1, device_id=other, device_id_type=MESH)

    out = lax.broadcasted_iota(jnp.int32, (256, 256), 0)
    src = lax.broadcasted_iota(jnp.int32, (256, 256), 1)
    first, second, third = out >> 4, (out >> 2) & 3, out & 3
    t1[...] = (src == second * 64 + first * 4 + third).astype(F32).astype(BF16)
    quarter = SIZE // XC
    first_of_z = y * (Z * XC) + z * XC
    up, down = lax.rem(me + N - 1, N), lax.rem(me + 1, N)
    up_z, down_z = lax.rem(first_of_z + N - 1, N), lax.rem(first_of_z + XC, N)
    ways = (
        (0, ROWS - 1, 0, XC - 1, down, down_z),
        (1, 0, ROWS + 1, 0, up, up_z),
    )

    def halo_copy(way, source, cols, sem, to):
        return pltpu.make_async_remote_copy(
            src_ref=source,
            dst_ref=cotp.at[ways[way][2], cols, :],
            send_sem=sem,
            recv_sem=halo_recv.at[way],
            device_id=device(to),
            device_id_type=MESH,
        )

    def halo_whole(way):
        _, row, _, _, to, _ = ways[way]
        return halo_copy(way, cot_h.at[row], pl.ds(EDGE, SIZE), halo_send.at[way], to)

    def halo_own(way):
        _, row, _, end, to, _ = ways[way]
        source = cot_h.at[row, pl.ds(end * quarter, quarter), :]
        return halo_copy(way, source, pl.ds(EDGE + end * quarter, quarter), halo_send.at[way], to)

    def halo_hand(way, k):
        row = ways[way][1]
        return pltpu.make_async_remote_copy(
            src_ref=cot_h.at[row, pl.ds(k * quarter, quarter), :],
            dst_ref=relay.at[way],
            send_sem=hand_send.at[way],
            recv_sem=hand_recv.at[way],
            device_id=(y, z * XC + k, h),
            device_id_type=MESH,
        )

    def halo_pass(way):
        cols = pl.ds(aligned(EDGE + xc * quarter, EDGE), quarter)
        return halo_copy(way, relay.at[way], cols, pass_send.at[way], ways[way][5])

    def halo_start():
        for way, _, _, end, _, _ in ways:

            @pl.when(xc == end)
            def _():
                for k in range(XC):
                    if k != end:
                        halo_hand(way, k).start()
                halo_own(way).start()

            @pl.when(xc != end)
            def _():
                halo_whole(way).start()

    def halo_forward():
        for way, _, _, end, _, _ in ways:

            @pl.when(xc != end)
            def _():
                pltpu.make_async_copy(relay.at[way], relay.at[way], hand_recv.at[way]).wait()
                halo_pass(way).start()

    def halo_got():
        for way, _, row, _, _, _ in ways:
            part = cotp.at[row, pl.ds(EDGE, SIZE), :]
            pltpu.make_async_copy(part, part, halo_recv.at[way]).wait()

    def halo_sent():
        for way, _, _, end, _, _ in ways:

            @pl.when(xc == end)
            def _():
                part = cotp.at[0, pl.ds(EDGE, (XC - 1) * quarter), :]
                pltpu.make_async_copy(part, part, hand_send.at[way]).wait()
                halo_own(way).wait_send()

            @pl.when(xc != end)
            def _():
                halo_whole(way).wait_send()
                halo_pass(way).wait_send()

    def pack(band, parts, buf):
        for half in range(2):
            stack = jnp.concatenate([p[64 * half : 64 * half + 64] for p in parts], axis=0)
            at = aligned(band * (Z * XC * CELL) + half * 256, 256)
            buf[pl.ds(at, 256), :] = dot(t1[...], stack).astype(BF16)

    def send(dy, buf, dst, k, sems):
        band = lax.rem(y + dy, Y)
        mine = aligned(me * CELL, CELL)

        @pl.when(dy == 0)
        def _():
            pltpu.make_async_copy(
                buf.at[pl.ds(mine, CELL), :], dst.at[pl.ds(mine, CELL), :], sems(0)
            ).start()

        def one(i, carry):
            par = i // 16
            dz = lax.rem(i // 4, 4) * 2 + par
            t = band * (Z * XC) + lax.rem(z + dz, Z) * XC + lax.rem(xc + i, XC)
            pltpu.make_async_remote_copy(
                src_ref=buf.at[pl.ds(aligned(t * CELL, CELL), CELL), :],
                dst_ref=dst.at[pl.ds(mine, CELL), :],
                send_sem=send_sem.at[k],
                recv_sem=sems(dy * 2 + par),
                device_id=device(t),
                device_id_type=MESH,
            ).start()
            return carry

        lax.fori_loop(jnp.where(dy == 0, 1, 0), Z * XC, one, 0)

    def wait_sent(buf, k):
        part = buf.at[pl.ds(0, (N - 1) * CELL), :]
        pltpu.make_async_copy(part, part, send_sem.at[k]).wait()

    def wait_got(buf, k):
        pltpu.make_async_copy(buf, buf, recv_sem.at[k]).wait()

    def unpack(buf, dst):
        def one(b, carry):
            block = dot(t2[...], buf[pl.ds(aligned(b * 256, 256), 256), :]).astype(BF16)
            for w in range(ROWS):
                dst[w, pl.ds(aligned(b * 64, 64), 64), :] = block[64 * w : 64 * w + 64]
            return carry

        lax.fori_loop(0, N * CELL // 256, one, 0)

    def band_of(dy):
        band = lax.rem(y + dy, Y)
        return band, pl.ds(aligned(band * BAND, BAND), BAND)

    pl.semaphore_wait(barrier, N)
    halo_start()

    loads[0].wait()
    loads[1].wait()
    loads[2].start()
    loads[3].start()

    def mix_rows(dy, carry):
        band, cols = band_of(dy)
        pack(band, [dot(rf[q, cols, :], tok[q]).astype(BF16) for q in range(ROWS)], s1)
        return carry

    def send_rows(dy, carry):
        send(dy, s1, r1, 0, lambda g: recv_sem.at[0])
        return carry

    mix_rows(jnp.int32(0), 0)
    send_rows(jnp.int32(0), 0)
    halo_forward()

    def mix_and_send(dy, carry):
        mix_rows(dy, carry)
        return send_rows(dy, carry)

    lax.fori_loop(1, Y, mix_and_send, 0)

    first, second, third = out >> 6, (out >> 2) & 15, out & 3
    t2[...] = (src == second * 16 + third * 4 + first).astype(F32).astype(BF16)
    cotp[:, 0:EDGE, :] = jnp.zeros((ROWS + 2, EDGE, SIZE), BF16)
    cotp[:, EDGE + SIZE :, :] = jnp.zeros((ROWS + 2, EDGE, SIZE), BF16)
    for i in range(3):
        kf[3 * i : 3 * i + 3, :] = kern[i].astype(F32)
    taps[...] = jnp.zeros_like(taps)

    loads[2].wait()
    halo_got()

    @pl.when(me == 0)
    def _():
        cotp[0, EDGE : EDGE + SIZE, :] = jnp.zeros((SIZE, SIZE), BF16)

    @pl.when(me == N - 1)
    def _():
        cotp[ROWS + 1, EDGE : EDGE + SIZE, :] = jnp.zeros((SIZE, SIZE), BF16)

    parts = SIZE // STEP

    def tile(it):
        r = it // (parts * parts)
        at = aligned(lax.rem(it // parts, parts) * STEP, STEP)
        lanes = pl.ds(aligned(lax.rem(it, parts) * STEP, STEP), STEP)
        wide = pl.ds(at, STEP + 2 * EDGE)
        return r, pl.ds(at, STEP), wide, lanes

    inner = slice(EDGE, EDGE + STEP)
    span = STEP + 2 * EDGE

    def shifted(x):
        return (pltpu.roll(x, span - 1, 0)[inner], x[inner], pltpu.roll(x, 1, 0)[inner])

    def conv(it, carry):
        r, cols, wide, lanes = tile(it)
        rows = [cotp[r + 2 - i, wide, lanes].astype(F32) for i in range(3)]
        sums = []
        for j in range(3):
            term = rows[0] * kf[j : j + 1, lanes]
            for i in (1, 2):
                term = term + rows[i] * kf[3 * i + j : 3 * i + j + 1, lanes]
            sums.append(term)
        grad = (
            pltpu.roll(sums[0], span - 1, 0)[inner]
            + sums[1][inner]
            + pltpu.roll(sums[2], 1, 0)[inner]
        )
        gate = jax.nn.sigmoid(tok[r, cols, lanes].astype(F32))
        grad = grad * gate
        mid[r, cols, lanes] = grad.astype(BF16)
        hold[r, cols, lanes] = grad * (1.0 - gate)
        return carry

    lax.fori_loop(0, ROWS * parts * parts, conv, 0)

    def send_grad(dy, carry):
        band, cols = band_of(dy)
        pack(band, [mid[q, cols, :] for q in range(ROWS)], s2)
        send(dy, s2, r2, 1, lambda g: recv_sem.at[1])
        return carry

    lax.fori_loop(0, Y, send_grad, 0)

    loads[3].wait()
    wait_got(r1, 0)
    unpack(r1, xs)
    wait_sent(s1, 0)

    def mix_columns(dy, carry):
        band, cols = band_of(dy)
        pack(band, [dot(cf[q, cols, :], xs[q]).astype(BF16) for q in range(ROWS)], s1)
        send(dy, s1, r3, 2, lambda g: recv_sem.at[2])
        return carry

    lax.fori_loop(0, Y, mix_columns, 0)

    wait_got(r2, 1)
    unpack(r2, gs)
    wait_sent(s2, 1)

    def back_columns(dy, carry):
        band, cols = band_of(dy)
        pack(
            band,
            [dot(cf[q, :, cols], gs[q], ((0,), (0,))).astype(BF16) for q in range(ROWS)],
            s2,
        )
        return carry

    def send_back(dy, carry):
        send(dy, s2, r4, 3, lambda g: last_sem.at[g])
        return carry

    lax.fori_loop(0, Y, back_columns, 0)
    lax.fori_loop(0, Y // 2, send_back, 0)

    def half_of(which):
        return pl.ds(aligned(which * (SIZE // 2), SIZE // 2), SIZE // 2)

    def column_copy(q):
        return pltpu.make_async_remote_copy(
            src_ref=col_out.at[q],
            dst_ref=col_got.at[q],
            send_sem=col_send.at[q],
            recv_sem=col_recv.at[q],
            device_id=other,
            device_id_type=MESH,
        )

    def column_away(q, carry):
        col_out[q] = dot(gs[q, half_of(1 - h), :], xs[q], ((1,), (1,))).astype(BF16)
        column_copy(q).start()
        return carry

    lax.fori_loop(0, ROWS, column_away, 0)

    wait_got(r3, 2)
    unpack(r3, mid)

    def gated(it, carry):
        r, cols, wide, lanes = tile(it)
        mixed = mid[r, cols, lanes].astype(F32)
        gate = jax.nn.sigmoid(tok[r, cols, lanes].astype(F32))
        cells = (mixed * gate).astype(BF16).astype(F32)
        hold[r, cols, lanes] = hold[r, cols, lanes] * mixed
        for i in range(3):
            row = cotp[r + 2 - i, wide, lanes].astype(F32)
            for j, moved in enumerate(shifted(row)):
                term = (cells * moved).reshape(STEP // 8, 8, STEP)
                taps[3 * i + j, :, lanes] += jnp.sum(term, axis=0)
        return carry

    lax.fori_loop(0, ROWS * parts * parts, gated, 0)

    steps = (
        (Z, 0, lambda i: (y, lax.rem(z + i, Z) * XC + xc, h)),
        (Y, Z - 1, lambda i: (lax.rem(y + i, Y), tk, h)),
        (XC, Z + Y - 2, lambda i: (y, z * XC + lax.rem(xc + i, XC), h)),
    )

    def sum_start(k):
        size, slot, peer = steps[k]
        for i in range(1, size):
            pltpu.make_async_remote_copy(
                src_ref=total.at[k],
                dst_ref=held.at[slot + i - 1],
                send_sem=sum_send.at[k],
                recv_sem=sum_recv.at[k],
                device_id=peer(i),
                device_id_type=MESH,
            ).start()

    def sum_finish(k):
        size, slot, _ = steps[k]
        part = held.at[pl.ds(slot, size - 1)]
        pltpu.make_async_copy(part, part, sum_recv.at[k]).wait()
        total[k + 1] = total[k] + jnp.sum(held[slot : slot + size - 1], axis=0)

    def sum_sent(k):
        size, slot, _ = steps[k]
        part = held.at[pl.ds(slot, size - 1)]
        pltpu.make_async_copy(part, part, sum_send.at[k]).wait()

    total[0] = jnp.zeros((16, SIZE), F32)
    for k in range(9):
        total[0, k : k + 1, :] = jnp.sum(taps[k], axis=0, keepdims=True)
    sum_start(0)
    lax.fori_loop(Y // 2, Y, send_back, 0)

    def column_store(q):
        return pltpu.make_async_copy(col_done.at[q], gcol_h.at[q], store_sem.at[q])

    def column_here(q, carry):
        term = dot(gs[q, half_of(h), :], xs[q], ((1,), (1,)))
        column_copy(q).wait_recv()
        col_done[q] = (term + col_got[q].astype(F32)).astype(BF16)
        column_store(q).start()
        return carry

    def source(dy):
        band = lax.rem(y + Y - dy, Y)
        cols = pl.ds(aligned(band * BAND, BAND), BAND)
        return band, cols, band // 2 != h, aligned(lax.rem(band, 2) * BAND, BAND)

    def row_copy(at):
        part = pl.ds(at, 16)
        return pltpu.make_async_remote_copy(
            src_ref=row_out.at[:, part, :],
            dst_ref=row_got.at[:, part, :],
            send_sem=row_send.at[at // BAND],
            recv_sem=row_recv.at[at // BAND],
            device_id=other,
            device_id_type=MESH,
        )

    def row_store(slot):
        part = pl.ds(slot * BAND, BAND)
        return pltpu.make_async_copy(
            row_done.at[:, part, :], grow_h.at[:, part, :], store_sem.at[ROWS + slot]
        )

    def row_here(dy):
        band, cols, away, base = source(dy)

        @pl.when(jnp.logical_not(away))
        def _():
            part = pl.ds(base, BAND)
            got = row_got.at[:, part, :]
            terms = [dot(grows[q, cols, :], tok[q], ((1,), (1,))) for q in range(ROWS)]
            pltpu.make_async_copy(got, got, row_recv.at[base // BAND]).wait()
            for q in range(ROWS):
                row_done[q, part, :] = (terms[q] + row_got[q, part, :].astype(F32)).astype(BF16)
            row_store(base // BAND).start()

    def arrive(dy, par):
        band, cols, away, base = source(dy)
        g = dy * 2 + par
        part = r4.at[pl.ds(0, 256), :]
        pltpu.make_async_copy(part, part, last_sem.at[g]).wait()
        zp = lax.rem(z + par, 2)
        blocks = [r4[pl.ds(aligned((band * Z + zp + 2 * m) * 64, 64), 64), :] for m in range(4)]
        block = dot(t2[...], jnp.concatenate(blocks, axis=0)).astype(BF16)
        for q in range(ROWS):
            for m in range(4):
                at = aligned(band * BAND + (zp + 2 * m) * 16, 16)
                low = 64 * q + 16 * m
                grows[q, pl.ds(at, 16), :] = block[low : low + 16]

        @pl.when(away)
        def _():
            for q in range(ROWS):
                term = dot(block[64 * q : 64 * q + 64], tok[q], ((1,), (1,))).astype(BF16)
                for m in range(4):
                    at = aligned(base + (zp + 2 * m) * 16, 16)
                    row_out[q, pl.ds(at, 16), :] = term[16 * m : 16 * m + 16]
            for m in range(4):
                row_copy(aligned(base + (zp + 2 * m) * 16, 16)).start()

    def back(dy, q):
        cols = source(dy)[1]
        return hold[q] + dot(rf[q, cols, :], grows[q, cols, :], ((0,), (0,)))

    def token_store(q):
        return pltpu.make_async_copy(mid.at[q], gtok_h.at[q], store_sem.at[ROWS + 2 + q])

    for dy in range(Y):
        arrive(dy, 0)
        if dy == 3:
            row_here(0)
        arrive(dy, 1)
        for q in range(ROWS):
            if dy < 3:
                hold[q] = back(dy, q)
            else:
                mid[q] = back(dy, q).astype(BF16)
                token_store(q).start()
        if dy == 0:
            lax.fori_loop(0, ROWS, column_here, 0)
        if dy == 1:
            sum_finish(0)
            sum_start(1)
        if dy == 2:
            sum_finish(1)
            sum_start(2)
        if dy == 3:
            row_here(1)
            row_here(2)
            sum_finish(2)
            for i in range(3):
                gkern[i] = total[3, 3 * i : 3 * i + 3, :]
            row_here(3)

    wait_sent(s1, 2)
    wait_sent(s2, 3)
    halo_sent()
    for k in range(3):
        sum_sent(k)
    for slot in range(2):
        part = row_out.at[:, pl.ds(slot * BAND, BAND), :]
        pltpu.make_async_copy(part, part, row_send.at[slot]).wait()
        row_store(slot).wait()
    for q in range(ROWS):
        column_copy(q).wait_send()
        column_store(q).wait()
        token_store(q).wait()


def shards(tokens, row_factor, column_factor, kernel, cotangent):
    full = (ROWS, SIZE, SIZE)
    half = (ROWS, SIZE // 2, SIZE)
    flat = (N * CELL, SIZE)
    vmem, dma = pltpu.VMEM, pltpu.SemaphoreType.DMA
    whole = pl.BlockSpec(memory_space=pl.ANY)
    local = pl.BlockSpec(memory_space=pltpu.VMEM)
    return pl.pallas_call(
        mixer,
        out_shape=[
            jax.ShapeDtypeStruct(full, BF16),
            jax.ShapeDtypeStruct(half, BF16),
            jax.ShapeDtypeStruct(half, BF16),
            jax.ShapeDtypeStruct((3, 3, SIZE), F32),
        ],
        in_specs=[whole, whole, whole, local, whole],
        out_specs=[whole, whole, whole, local],
        scratch_shapes=[
            vmem(full, BF16), vmem(full, BF16), vmem(full, BF16),
            vmem((ROWS + 2, SIZE + 2 * EDGE, SIZE), BF16),
            vmem(flat, BF16), vmem(flat, BF16),
            vmem(flat, BF16), vmem(flat, BF16), vmem(flat, BF16), vmem(flat, BF16),
            vmem(full, BF16), vmem(full, BF16), vmem(full, F32), vmem(full, BF16), vmem(full, BF16),
            vmem(half, BF16), vmem(half, BF16), vmem(half, BF16), vmem(half, BF16),
            vmem(half, BF16), vmem(half, BF16),
            vmem((2, SIZE // XC, SIZE), BF16), vmem((9, 8, SIZE), F32), vmem((16, SIZE), F32),
            vmem((4, 16, SIZE), F32), vmem((Z + Y + XC - 3, 16, SIZE), F32),
            vmem((256, 256), BF16), vmem((256, 256), BF16),
            dma((4,)), dma((2,)), dma((2,)), dma((2,)), dma((2,)), dma((2,)), dma((4,)), dma((3,)), dma((2 * Y,)),
            dma((ROWS,)), dma((ROWS,)), dma((2,)), dma((2,)), dma((3,)), dma((3,)),
            dma((2 * ROWS + 2,)),
        ],
        name="mixer",
        compiler_params=pltpu.CompilerParams(
            collective_id=1, has_side_effects=True, vmem_limit_bytes=49 * 2**20
        ),
        cost_estimate=pl.CostEstimate(
            flops=7 * 10**9, bytes_accessed=12 * 2**20, transcendentals=4 * 10**6
        ),
    )(tokens, row_factor, column_factor, kernel, cotangent)


def solution(mesh):
    return jax.shard_map(
        lambda *args: tuple(shards(*args)),
        mesh=mesh,
        in_specs=(
            P(("grp", "tok"), None, "ch"),
            P(("grp", "tok"), None, None),
            P(("grp", "tok"), None, None),
            P(None, None, "ch"),
            P(("grp", "tok"), None, "ch"),
        ),
        out_specs=(
            P(("grp", "tok"), None, "ch"),
            P(("grp", "tok"), "ch", None),
            P(("grp", "tok"), "ch", None),
            P(None, None, "ch"),
        ),
        check_vma=False,
    )
```

```python
import jax
import jax.numpy as jnp
from jax import lax
from jax.experimental import pallas as pl
from jax.experimental.pallas import tpu as pltpu
from jax.sharding import PartitionSpec as P

MESH = pl.DeviceIdType.MESH
F32, BF16 = jnp.float32, jnp.bfloat16
Y, Z, XC = 4, 8, 4
N = Y * Z * XC
ROWS = 4
SIZE = 512
CELL = ROWS * ROWS
BAND = SIZE // Y
EDGE = 16
STEP = 128


def dot(a, b, contract=((1,), (0,))):
    return lax.dot_general(a, b, (contract, ((), ())), preferred_element_type=F32)


def aligned(value, multiple):
    return pl.multiple_of(value, multiple)


def mixer(
    tok_h, rf_h, cf_h, kern, cot_h,
    gtok_h, grow_h, gcol_h, gkern,
    tok, rf, cf, cotp, s1, s2, r1, r2, r3, r4, xs, gs, hold, mid, grows,
    row_out, col_out, row_got, col_got, row_done, col_done, relay, taps, kf, total, held, t1, t2, t3,
    load_sem, halo_send, halo_recv, hand_send, hand_recv, pass_send, send_sem, recv_sem, last_sem,
    col_send, col_recv, row_send, row_recv, sum_send, sum_recv, store_sem,
):
    y, tk, h = lax.axis_index("grp"), lax.axis_index("tok"), lax.axis_index("ch")
    z, xc = tk // XC, lax.rem(tk, XC)
    me = y * (Z * XC) + tk
    other = (y, tk, 1 - h)

    def device(t):
        return (lax.div(t, Z * XC), lax.rem(t, Z * XC), h)

    loads = [
        pltpu.make_async_copy(tok_h, tok, load_sem.at[0]),
        pltpu.make_async_copy(rf_h, rf, load_sem.at[1]),
        pltpu.make_async_copy(cot_h, cotp.at[pl.ds(1, ROWS), pl.ds(EDGE, SIZE), :], load_sem.at[2]),
        pltpu.make_async_copy(cf_h, cf, load_sem.at[3]),
    ]
    for load in loads[:2]:
        load.start()

    barrier = pltpu.get_barrier_semaphore()

    for dy in range(Y):
        band = lax.rem(y + dy, Y)

        def greet(i, carry):
            to = (band, lax.rem(tk + i, Z * XC), h)
            pl.semaphore_signal(barrier, inc=1, device_id=to, device_id_type=MESH)
            return carry

        lax.fori_loop(1 if dy == 0 else 0, Z * XC, greet, 0)
    pl.semaphore_signal(barrier, inc=1, device_id=other, device_id_type=MESH)

    out = lax.broadcasted_iota(jnp.int32, (256, 256), 0)
    src = lax.broadcasted_iota(jnp.int32, (256, 256), 1)
    first, second, third = out >> 4, (out >> 2) & 3, out & 3
    t1[...] = (src == second * 64 + first * 4 + third).astype(F32).astype(BF16)
    quarter = SIZE // XC
    first_of_z = y * (Z * XC) + z * XC
    up, down = lax.rem(me + N - 1, N), lax.rem(me + 1, N)
    up_z, down_z = lax.rem(first_of_z + N - 1, N), lax.rem(first_of_z + XC, N)
    ways = (
        (0, ROWS - 1, 0, XC - 1, down, down_z),
        (1, 0, ROWS + 1, 0, up, up_z),
    )

    def halo_copy(way, source, cols, sem, to):
        return pltpu.make_async_remote_copy(
            src_ref=source,
            dst_ref=cotp.at[ways[way][2], cols, :],
            send_sem=sem,
            recv_sem=halo_recv.at[way],
            device_id=device(to),
            device_id_type=MESH,
        )

    def halo_whole(way):
        _, row, _, _, to, _ = ways[way]
        return halo_copy(way, cot_h.at[row], pl.ds(EDGE, SIZE), halo_send.at[way], to)

    def halo_own(way):
        _, row, _, end, to, _ = ways[way]
        source = cot_h.at[row, pl.ds(end * quarter, quarter), :]
        return halo_copy(way, source, pl.ds(EDGE + end * quarter, quarter), halo_send.at[way], to)

    def halo_hand(way, k):
        row = ways[way][1]
        return pltpu.make_async_remote_copy(
            src_ref=cot_h.at[row, pl.ds(k * quarter, quarter), :],
            dst_ref=relay.at[way],
            send_sem=hand_send.at[way],
            recv_sem=hand_recv.at[way],
            device_id=(y, z * XC + k, h),
            device_id_type=MESH,
        )

    def halo_pass(way):
        cols = pl.ds(aligned(EDGE + xc * quarter, EDGE), quarter)
        return halo_copy(way, relay.at[way], cols, pass_send.at[way], ways[way][5])

    def halo_start():
        for way, _, _, end, _, _ in ways:

            @pl.when(xc == end)
            def _():
                for k in range(XC):
                    if k != end:
                        halo_hand(way, k).start()
                halo_own(way).start()

    def halo_forward():
        for way, _, _, end, _, _ in ways:

            @pl.when(xc != end)
            def _():
                pltpu.make_async_copy(relay.at[way], relay.at[way], hand_recv.at[way]).wait()
                halo_pass(way).start()
                halo_whole(way).start()

    def halo_got():
        for way, _, row, _, _, _ in ways:
            part = cotp.at[row, pl.ds(EDGE, SIZE), :]
            pltpu.make_async_copy(part, part, halo_recv.at[way]).wait()

    def halo_sent():
        for way, _, _, end, _, _ in ways:

            @pl.when(xc == end)
            def _():
                part = cotp.at[0, pl.ds(EDGE, (XC - 1) * quarter), :]
                pltpu.make_async_copy(part, part, hand_send.at[way]).wait()
                halo_own(way).wait_send()

            @pl.when(xc != end)
            def _():
                halo_whole(way).wait_send()
                halo_pass(way).wait_send()

    def pack(band, parts, buf):
        for half in range(2):
            stack = jnp.concatenate([p[64 * half : 64 * half + 64] for p in parts], axis=0)
            at = aligned(band * (Z * XC * CELL) + half * 256, 256)
            buf[pl.ds(at, 256), :] = dot(t1[...], stack).astype(BF16)

    def offset(pair, which):
        first = jnp.where(pair == 0, 0, jnp.where(pair == 1, 2, jnp.where(pair == 2, 3, 1)))
        second = jnp.where(pair == 0, 4, jnp.where(pair == 1, 6, jnp.where(pair == 2, 5, 7)))
        return jnp.where(which == 0, first, second), pair

    def send(dy, buf, dst, k, sems):
        band = lax.rem(y + dy, Y)
        mine = aligned(me * CELL, CELL)

        @pl.when(dy == 0)
        def _():
            pltpu.make_async_copy(
                buf.at[pl.ds(mine, CELL), :], dst.at[pl.ds(mine, CELL), :], sems(0)
            ).start()

        def one(n, carry):
            dz, group = offset(lax.div(n, 2), lax.rem(n, 2))
            to_z = lax.rem(z + dz, Z)
            for i in range(XC):
                to = to_z * XC + lax.rem(xc + i, XC)

                def go():
                    at = aligned((band * (Z * XC) + to) * CELL, CELL)
                    pltpu.make_async_remote_copy(
                        src_ref=buf.at[pl.ds(at, CELL), :],
                        dst_ref=dst.at[pl.ds(mine, CELL), :],
                        send_sem=send_sem.at[k],
                        recv_sem=sems(dy * 4 + group),
                        device_id=(band, to, h),
                        device_id_type=MESH,
                    ).start()

                if i == 0:
                    pl.when(jnp.logical_or(dy > 0, n > 0))(go)
                else:
                    go()
            return carry

        lax.fori_loop(0, Z, one, 0)

    def wait_sent(buf, k):
        part = buf.at[pl.ds(0, (N - 1) * CELL), :]
        pltpu.make_async_copy(part, part, send_sem.at[k]).wait()

    def wait_got(buf, k):
        pltpu.make_async_copy(buf, buf, recv_sem.at[k]).wait()

    def unpack(buf, dst):
        def one(b, carry):
            block = dot(t2[...], buf[pl.ds(aligned(b * 256, 256), 256), :]).astype(BF16)
            for w in range(ROWS):
                dst[w, pl.ds(aligned(b * 64, 64), 64), :] = block[64 * w : 64 * w + 64]
            return carry

        lax.fori_loop(0, N * CELL // 256, one, 0)

    def band_of(dy):
        band = lax.rem(y + dy, Y)
        return band, pl.ds(aligned(band * BAND, BAND), BAND)

    pl.semaphore_wait(barrier, N)
    halo_start()

    loads[0].wait()
    loads[1].wait()
    for load in loads[2:]:
        load.start()

    def mix_rows(dy, carry):
        band, cols = band_of(dy)
        pack(band, [dot(rf[q, cols, :], tok[q]).astype(BF16) for q in range(ROWS)], s1)
        return carry

    def send_rows(dy, carry):
        send(dy, s1, r1, 0, lambda g: recv_sem.at[0])
        return carry

    def mix_and_send(dy, carry):
        mix_rows(dy, carry)
        return send_rows(dy, carry)

    mix_and_send(jnp.int32(0), 0)
    halo_forward()
    lax.fori_loop(1, Y, mix_and_send, 0)

    first, second, third = out >> 6, (out >> 2) & 15, out & 3
    t2[...] = (src == second * 16 + third * 4 + first).astype(F32).astype(BF16)
    out, src = out[:128, :128], src[:128, :128]
    first, second, third = out >> 5, (out >> 2) & 7, out & 3
    t3[...] = (src == second * 16 + third * 4 + first).astype(F32).astype(BF16)
    cotp[:, 0:EDGE, :] = jnp.zeros((ROWS + 2, EDGE, SIZE), BF16)
    cotp[:, EDGE + SIZE :, :] = jnp.zeros((ROWS + 2, EDGE, SIZE), BF16)
    for i in range(3):
        kf[3 * i : 3 * i + 3, :] = kern[i].astype(F32)
    taps[...] = jnp.zeros_like(taps)

    loads[2].wait()
    halo_got()

    @pl.when(me == 0)
    def _():
        cotp[0, EDGE : EDGE + SIZE, :] = jnp.zeros((SIZE, SIZE), BF16)

    @pl.when(me == N - 1)
    def _():
        cotp[ROWS + 1, EDGE : EDGE + SIZE, :] = jnp.zeros((SIZE, SIZE), BF16)

    parts = SIZE // STEP

    def tile(it):
        r = it // (parts * parts)
        at = aligned(lax.rem(it // parts, parts) * STEP, STEP)
        lanes = pl.ds(aligned(lax.rem(it, parts) * STEP, STEP), STEP)
        wide = pl.ds(at, STEP + 2 * EDGE)
        return r, pl.ds(at, STEP), wide, lanes

    inner = slice(EDGE, EDGE + STEP)
    span = STEP + 2 * EDGE

    def shifted(x):
        return (pltpu.roll(x, span - 1, 0)[inner], x[inner], pltpu.roll(x, 1, 0)[inner])

    def conv(it, carry):
        r, cols, wide, lanes = tile(it)
        rows = [cotp[r + 2 - i, wide, lanes].astype(F32) for i in range(3)]
        sums = []
        for j in range(3):
            term = rows[0] * kf[j : j + 1, lanes]
            for i in (1, 2):
                term = term + rows[i] * kf[3 * i + j : 3 * i + j + 1, lanes]
            sums.append(term)
        grad = (
            pltpu.roll(sums[0], span - 1, 0)[inner]
            + sums[1][inner]
            + pltpu.roll(sums[2], 1, 0)[inner]
        )
        gate = jax.nn.sigmoid(tok[r, cols, lanes].astype(F32))
        grad = grad * gate
        mid[r, cols, lanes] = grad.astype(BF16)
        hold[r, cols, lanes] = grad * (1.0 - gate)
        return carry

    lax.fori_loop(0, ROWS * parts * parts, conv, 0)

    def send_grad(dy, carry):
        band, cols = band_of(dy)
        pack(band, [mid[q, cols, :] for q in range(ROWS)], s2)
        send(dy, s2, r2, 1, lambda g: recv_sem.at[1])
        return carry

    lax.fori_loop(0, Y, send_grad, 0)

    loads[3].wait()
    wait_got(r1, 0)
    unpack(r1, xs)
    wait_sent(s1, 0)

    def mix_columns(dy, carry):
        band, cols = band_of(dy)
        pack(band, [dot(cf[q, cols, :], xs[q]).astype(BF16) for q in range(ROWS)], s1)
        send(dy, s1, r3, 2, lambda g: recv_sem.at[2])
        return carry

    lax.fori_loop(0, Y, mix_columns, 0)

    wait_got(r2, 1)
    unpack(r2, gs)
    wait_sent(s2, 1)

    def back_columns(dy, carry):
        band, cols = band_of(dy)
        pack(
            band,
            [dot(cf[q, :, cols], gs[q], ((0,), (0,))).astype(BF16) for q in range(ROWS)],
            s2,
        )
        return carry

    def turn(i):
        return i % 2 * 2 + i // 2 if isinstance(i, int) else lax.rem(i, 2) * 2 + lax.div(i, 2)

    def send_back(i, carry):
        send(turn(i), s2, r4, 3, lambda g: last_sem.at[g])
        return carry

    lax.fori_loop(0, Y, back_columns, 0)
    lax.fori_loop(0, Y // 2, send_back, 0)

    def half_of(which):
        return pl.ds(aligned(which * (SIZE // 2), SIZE // 2), SIZE // 2)

    def column_copy(q):
        return pltpu.make_async_remote_copy(
            src_ref=col_out.at[q],
            dst_ref=col_got.at[q],
            send_sem=col_send.at[q],
            recv_sem=col_recv.at[q],
            device_id=other,
            device_id_type=MESH,
        )

    def column_away(q, carry):
        col_out[q] = dot(gs[q, half_of(1 - h), :], xs[q], ((1,), (1,))).astype(BF16)
        column_copy(q).start()
        return carry

    lax.fori_loop(0, ROWS, column_away, 0)

    wait_got(r3, 2)
    unpack(r3, mid)

    def gated(it, carry):
        r, cols, wide, lanes = tile(it)
        mixed = mid[r, cols, lanes].astype(F32)
        gate = jax.nn.sigmoid(tok[r, cols, lanes].astype(F32))
        cells = (mixed * gate).astype(BF16).astype(F32)
        hold[r, cols, lanes] = hold[r, cols, lanes] * mixed
        for i in range(3):
            row = cotp[r + 2 - i, wide, lanes].astype(F32)
            for j, moved in enumerate(shifted(row)):
                term = (cells * moved).reshape(STEP // 8, 8, STEP)
                taps[3 * i + j, :, lanes] += jnp.sum(term, axis=0)
        return carry

    lax.fori_loop(0, ROWS * parts * parts, gated, 0)

    steps = (
        (Z, 0, lambda i: (y, lax.rem(z + i, Z) * XC + xc, h)),
        (Y, Z - 1, lambda i: (lax.rem(y + i, Y), tk, h)),
        (XC, Z + Y - 2, lambda i: (y, z * XC + lax.rem(xc + i, XC), h)),
    )

    def sum_start(k):
        size, slot, peer = steps[k]
        for i in range(1, size):
            pltpu.make_async_remote_copy(
                src_ref=total.at[k],
                dst_ref=held.at[slot + i - 1],
                send_sem=sum_send.at[k],
                recv_sem=sum_recv.at[k],
                device_id=peer(i),
                device_id_type=MESH,
            ).start()

    def sum_finish(k):
        size, slot, _ = steps[k]
        part = held.at[pl.ds(slot, size - 1)]
        pltpu.make_async_copy(part, part, sum_recv.at[k]).wait()
        total[k + 1] = total[k] + jnp.sum(held[slot : slot + size - 1], axis=0)

    def sum_sent(k):
        size, slot, _ = steps[k]
        part = held.at[pl.ds(slot, size - 1)]
        pltpu.make_async_copy(part, part, sum_send.at[k]).wait()

    total[0] = jnp.zeros((16, SIZE), F32)
    for k in range(9):
        total[0, k : k + 1, :] = jnp.sum(taps[k], axis=0, keepdims=True)
    sum_start(0)
    lax.fori_loop(Y // 2, Y, send_back, 0)

    def column_store(q):
        return pltpu.make_async_copy(col_done.at[q], gcol_h.at[q], store_sem.at[q])

    def column_here(q, carry):
        term = dot(gs[q, half_of(h), :], xs[q], ((1,), (1,)))
        column_copy(q).wait_recv()
        col_done[q] = (term + col_got[q].astype(F32)).astype(BF16)
        column_store(q).start()
        return carry

    def source(dy):
        band = lax.rem(y + Y - dy, Y)
        cols = pl.ds(aligned(band * BAND, BAND), BAND)
        return band, cols, band // 2 != h, aligned(lax.rem(band, 2) * BAND, BAND)

    def row_copy(at):
        part = pl.ds(at, 16)
        return pltpu.make_async_remote_copy(
            src_ref=row_out.at[:, part, :],
            dst_ref=row_got.at[:, part, :],
            send_sem=row_send.at[at // BAND],
            recv_sem=row_recv.at[at // BAND],
            device_id=other,
            device_id_type=MESH,
        )

    def row_store(slot):
        part = pl.ds(slot * BAND, BAND)
        return pltpu.make_async_copy(
            row_done.at[:, part, :], grow_h.at[:, part, :], store_sem.at[ROWS + slot]
        )

    def row_here(dy):
        band, cols, away, base = source(dy)

        @pl.when(jnp.logical_not(away))
        def _():
            part = pl.ds(base, BAND)
            got = row_got.at[:, part, :]
            terms = [dot(grows[q, cols, :], tok[q], ((1,), (1,))) for q in range(ROWS)]
            pltpu.make_async_copy(got, got, row_recv.at[base // BAND]).wait()
            for q in range(ROWS):
                row_done[q, part, :] = (terms[q] + row_got[q, part, :].astype(F32)).astype(BF16)
            row_store(base // BAND).start()

    def arrive(dy, pair):
        band, cols, away, base = source(dy)
        part = r4.at[pl.ds(0, 128), :]
        pltpu.make_async_copy(part, part, last_sem.at[dy * 4 + pair]).wait()
        zs = [lax.rem(z + Z - dz, Z) for dz in ((0, 4), (2, 6), (3, 5), (1, 7))[pair]]
        blocks = [r4[pl.ds(aligned((band * Z + zz) * 64, 64), 64), :] for zz in zs]
        block = dot(t3[...], jnp.concatenate(blocks, axis=0)).astype(BF16)
        for q in range(ROWS):
            for m, zz in enumerate(zs):
                low = 32 * q + 16 * m
                grows[q, pl.ds(aligned(band * BAND + zz * 16, 16), 16), :] = block[low : low + 16]

        @pl.when(away)
        def _():
            for q in range(ROWS):
                term = dot(block[32 * q : 32 * q + 32], tok[q], ((1,), (1,))).astype(BF16)
                for m, zz in enumerate(zs):
                    at = aligned(base + zz * 16, 16)
                    row_out[q, pl.ds(at, 16), :] = term[16 * m : 16 * m + 16]
            for zz in zs:
                row_copy(aligned(base + zz * 16, 16)).start()

    def back(dy, q):
        cols = source(dy)[1]
        return hold[q] + dot(rf[q, cols, :], grows[q, cols, :], ((0,), (0,)))

    def token_store(q):
        return pltpu.make_async_copy(mid.at[q], gtok_h.at[q], store_sem.at[ROWS + 2 + q])

    for i in range(Y):
        dy = turn(i)
        for pair in range(4):
            arrive(dy, pair)
            if i == 3 and pair == 0:
                row_here(turn(0))
            if i == 3 and pair == 1:
                row_here(turn(1))
        for q in range(ROWS):
            if i < 3:
                hold[q] = back(dy, q)
            else:
                mid[q] = back(dy, q).astype(BF16)
                token_store(q).start()
        if i == 0:
            lax.fori_loop(0, ROWS, column_here, 0)
        if i == 1:
            sum_finish(0)
            sum_start(1)
        if i == 2:
            sum_finish(1)
            sum_start(2)
    row_here(turn(2))
    sum_finish(2)
    for i in range(3):
        gkern[i] = total[3, 3 * i : 3 * i + 3, :]
    row_here(turn(3))

    wait_sent(s1, 2)
    wait_sent(s2, 3)
    halo_sent()
    for k in range(3):
        sum_sent(k)
    for slot in range(2):
        part = row_out.at[:, pl.ds(slot * BAND, BAND), :]
        pltpu.make_async_copy(part, part, row_send.at[slot]).wait()
        row_store(slot).wait()
    for q in range(ROWS):
        column_copy(q).wait_send()
        column_store(q).wait()
        token_store(q).wait()


def shards(tokens, row_factor, column_factor, kernel, cotangent):
    full = (ROWS, SIZE, SIZE)
    half = (ROWS, SIZE // 2, SIZE)
    flat = (N * CELL, SIZE)
    vmem, dma = pltpu.VMEM, pltpu.SemaphoreType.DMA
    whole = pl.BlockSpec(memory_space=pl.ANY)
    local = pl.BlockSpec(memory_space=pltpu.VMEM)
    return pl.pallas_call(
        mixer,
        out_shape=[
            jax.ShapeDtypeStruct(full, BF16),
            jax.ShapeDtypeStruct(half, BF16),
            jax.ShapeDtypeStruct(half, BF16),
            jax.ShapeDtypeStruct((3, 3, SIZE), F32),
        ],
        in_specs=[whole, whole, whole, local, whole],
        out_specs=[whole, whole, whole, local],
        scratch_shapes=[
            vmem(full, BF16), vmem(full, BF16), vmem(full, BF16),
            vmem((ROWS + 2, SIZE + 2 * EDGE, SIZE), BF16),
            vmem(flat, BF16), vmem(flat, BF16),
            vmem(flat, BF16), vmem(flat, BF16), vmem(flat, BF16), vmem(flat, BF16),
            vmem(full, BF16), vmem(full, BF16), vmem(full, F32), vmem(full, BF16), vmem(full, BF16),
            vmem(half, BF16), vmem(half, BF16), vmem(half, BF16), vmem(half, BF16),
            vmem(half, BF16), vmem(half, BF16),
            vmem((2, SIZE // XC, SIZE), BF16), vmem((9, 8, SIZE), F32), vmem((16, SIZE), F32),
            vmem((4, 16, SIZE), F32), vmem((Z + Y + XC - 3, 16, SIZE), F32),
            vmem((256, 256), BF16), vmem((256, 256), BF16), vmem((128, 128), BF16),
            dma((4,)), dma((2,)), dma((2,)), dma((2,)), dma((2,)), dma((2,)), dma((4,)), dma((3,)), dma((4 * Y,)),
            dma((ROWS,)), dma((ROWS,)), dma((2,)), dma((2,)), dma((3,)), dma((3,)),
            dma((2 * ROWS + 2,)),
        ],
        name="mixer",
        compiler_params=pltpu.CompilerParams(
            collective_id=1, has_side_effects=True, vmem_limit_bytes=49 * 2**20
        ),
        cost_estimate=pl.CostEstimate(
            flops=7 * 10**9, bytes_accessed=12 * 2**20, transcendentals=4 * 10**6
        ),
    )(tokens, row_factor, column_factor, kernel, cotangent)


def solution(mesh):
    return jax.shard_map(
        lambda *args: tuple(shards(*args)),
        mesh=mesh,
        in_specs=(
            P(("grp", "tok"), None, "ch"),
            P(("grp", "tok"), None, None),
            P(("grp", "tok"), None, None),
            P(None, None, "ch"),
            P(("grp", "tok"), None, "ch"),
        ),
        out_specs=(
            P(("grp", "tok"), None, "ch"),
            P(("grp", "tok"), "ch", None),
            P(("grp", "tok"), "ch", None),
            P(None, None, "ch"),
        ),
        check_vma=False,
    )
```

```python
import jax
import jax.numpy as jnp
from jax import lax
from jax.experimental import pallas as pl
from jax.experimental.pallas import tpu as pltpu
from jax.sharding import PartitionSpec as P

MESH = pl.DeviceIdType.MESH
F32, BF16 = jnp.float32, jnp.bfloat16
Y, Z, XC = 4, 8, 4
N = Y * Z * XC
ROWS = 4
SIZE = 512
CELL = ROWS * ROWS
BAND = SIZE // Y
EDGE = 16
STEP = 128


def dot(a, b, contract=((1,), (0,))):
    return lax.dot_general(a, b, (contract, ((), ())), preferred_element_type=F32)


def aligned(value, multiple):
    return pl.multiple_of(value, multiple)


def mixer(
    tok_h, rf_h, cf_h, kern, cot_h,
    gtok_h, grow_h, gcol_h, gkern,
    tok, rf, cf, cotp, s1, s2, r1, r2, r3, r4, xs, gs, hold, mid, grows,
    row_out, col_out, row_got, col_got, row_done, col_done, relay, taps, kf, total, held, t1, t2, t3,
    load_sem, halo_send, halo_recv, hand_send, hand_recv, pass_send, send_sem, recv_sem, last_sem,
    col_send, col_recv, row_send, row_recv, sum_send, sum_recv, store_sem,
):
    y, tk, h = lax.axis_index("grp"), lax.axis_index("tok"), lax.axis_index("ch")
    z, xc = tk // XC, lax.rem(tk, XC)
    me = y * (Z * XC) + tk
    other = (y, tk, 1 - h)

    def device(t):
        return (lax.div(t, Z * XC), lax.rem(t, Z * XC), h)

    loads = [
        pltpu.make_async_copy(tok_h, tok, load_sem.at[0]),
        pltpu.make_async_copy(rf_h, rf, load_sem.at[1]),
        pltpu.make_async_copy(cot_h, cotp.at[pl.ds(1, ROWS), pl.ds(EDGE, SIZE), :], load_sem.at[2]),
        pltpu.make_async_copy(cf_h, cf, load_sem.at[3]),
    ]
    for load in loads[:2]:
        load.start()

    barrier = pltpu.get_barrier_semaphore()

    for dy in range(Y):
        band = lax.rem(y + dy, Y)

        def greet(i, carry):
            to = (band, lax.rem(tk + i, Z * XC), h)
            pl.semaphore_signal(barrier, inc=1, device_id=to, device_id_type=MESH)
            return carry

        lax.fori_loop(1 if dy == 0 else 0, Z * XC, greet, 0)
    pl.semaphore_signal(barrier, inc=1, device_id=other, device_id_type=MESH)

    out = lax.broadcasted_iota(jnp.int32, (256, 256), 0)
    src = lax.broadcasted_iota(jnp.int32, (256, 256), 1)
    first, second, third = out >> 4, (out >> 2) & 3, out & 3
    t1[...] = (src == second * 64 + first * 4 + third).astype(F32).astype(BF16)
    quarter = SIZE // XC
    first_of_z = y * (Z * XC) + z * XC
    up, down = lax.rem(me + N - 1, N), lax.rem(me + 1, N)
    up_z, down_z = lax.rem(first_of_z + N - 1, N), lax.rem(first_of_z + XC, N)
    ways = (
        (0, ROWS - 1, 0, XC - 1, down, down_z),
        (1, 0, ROWS + 1, 0, up, up_z),
    )

    def halo_copy(way, source, cols, sem, to):
        return pltpu.make_async_remote_copy(
            src_ref=source,
            dst_ref=cotp.at[ways[way][2], cols, :],
            send_sem=sem,
            recv_sem=halo_recv.at[way],
            device_id=device(to),
            device_id_type=MESH,
        )

    def halo_whole(way):
        _, row, _, _, to, _ = ways[way]
        return halo_copy(way, cot_h.at[row], pl.ds(EDGE, SIZE), halo_send.at[way], to)

    def halo_own(way):
        _, row, _, end, to, _ = ways[way]
        source = cot_h.at[row, pl.ds(end * quarter, quarter), :]
        return halo_copy(way, source, pl.ds(EDGE + end * quarter, quarter), halo_send.at[way], to)

    def halo_hand(way, k):
        row = ways[way][1]
        return pltpu.make_async_remote_copy(
            src_ref=cot_h.at[row, pl.ds(k * quarter, quarter), :],
            dst_ref=relay.at[way],
            send_sem=hand_send.at[way],
            recv_sem=hand_recv.at[way],
            device_id=(y, z * XC + k, h),
            device_id_type=MESH,
        )

    def halo_pass(way):
        cols = pl.ds(aligned(EDGE + xc * quarter, EDGE), quarter)
        return halo_copy(way, relay.at[way], cols, pass_send.at[way], ways[way][5])

    def halo_start():
        for way, _, _, end, _, _ in ways:

            @pl.when(xc == end)
            def _():
                for k in range(XC):
                    if k != end:
                        halo_hand(way, k).start()
                halo_own(way).start()

    def halo_forward():
        for way, _, _, end, _, _ in ways:

            @pl.when(xc != end)
            def _():
                pltpu.make_async_copy(relay.at[way], relay.at[way], hand_recv.at[way]).wait()
                halo_pass(way).start()
                halo_whole(way).start()

    def halo_got():
        for way, _, row, _, _, _ in ways:
            part = cotp.at[row, pl.ds(EDGE, SIZE), :]
            pltpu.make_async_copy(part, part, halo_recv.at[way]).wait()

    def halo_sent():
        for way, _, _, end, _, _ in ways:

            @pl.when(xc == end)
            def _():
                part = cotp.at[0, pl.ds(EDGE, (XC - 1) * quarter), :]
                pltpu.make_async_copy(part, part, hand_send.at[way]).wait()
                halo_own(way).wait_send()

            @pl.when(xc != end)
            def _():
                halo_whole(way).wait_send()
                halo_pass(way).wait_send()

    def pack(band, parts, buf):
        for half in range(2):
            stack = jnp.concatenate([p[64 * half : 64 * half + 64] for p in parts], axis=0)
            at = aligned(band * (Z * XC * CELL) + half * 256, 256)
            buf[pl.ds(at, 256), :] = dot(t1[...], stack).astype(BF16)

    def offset(pair, which):
        first = jnp.where(pair == 0, 0, jnp.where(pair == 1, 2, jnp.where(pair == 2, 3, 1)))
        second = jnp.where(pair == 0, 4, jnp.where(pair == 1, 6, jnp.where(pair == 2, 5, 7)))
        return jnp.where(which == 0, first, second)

    def send_self(buf, dst, sem):
        part = pl.ds(aligned(me * CELL, CELL), CELL)
        pltpu.make_async_copy(buf.at[part, :], dst.at[part, :], sem).start()

    def send_z(dy, dz, buf, dst, k, sem):
        band, to_z = lax.rem(y + dy, Y), lax.rem(z + dz, Z)
        for i in range(XC):
            to = to_z * XC + lax.rem(xc + i, XC)

            def go():
                at = aligned((band * (Z * XC) + to) * CELL, CELL)
                pltpu.make_async_remote_copy(
                    src_ref=buf.at[pl.ds(at, CELL), :],
                    dst_ref=dst.at[pl.ds(aligned(me * CELL, CELL), CELL), :],
                    send_sem=send_sem.at[k],
                    recv_sem=sem,
                    device_id=(band, to, h),
                    device_id_type=MESH,
                ).start()

            if i == 0:
                pl.when(jnp.logical_or(dy > 0, dz > 0))(go)
            else:
                go()

    def send(dy, buf, dst, k):
        @pl.when(dy == 0)
        def _():
            send_self(buf, dst, recv_sem.at[k])

        def one(n, carry):
            dz = offset(lax.div(n, 2), lax.rem(n, 2))
            send_z(dy, dz, buf, dst, k, recv_sem.at[k])
            return carry

        lax.fori_loop(0, Z, one, 0)

    def wait_sent(buf, k):
        part = buf.at[pl.ds(0, (N - 1) * CELL), :]
        pltpu.make_async_copy(part, part, send_sem.at[k]).wait()

    def wait_got(buf, k):
        pltpu.make_async_copy(buf, buf, recv_sem.at[k]).wait()

    def unpack(buf, dst):
        def one(b, carry):
            block = dot(t2[...], buf[pl.ds(aligned(b * 256, 256), 256), :]).astype(BF16)
            for w in range(ROWS):
                dst[w, pl.ds(aligned(b * 64, 64), 64), :] = block[64 * w : 64 * w + 64]
            return carry

        lax.fori_loop(0, N * CELL // 256, one, 0)

    def band_of(dy):
        band = lax.rem(y + dy, Y)
        return band, pl.ds(aligned(band * BAND, BAND), BAND)

    pl.semaphore_wait(barrier, N)
    halo_start()

    loads[0].wait()
    loads[1].wait()
    for load in loads[2:]:
        load.start()

    def mix_rows(dy, carry):
        band, cols = band_of(dy)
        pack(band, [dot(rf[q, cols, :], tok[q]).astype(BF16) for q in range(ROWS)], s1)
        return carry

    def send_rows(dy, carry):
        send(dy, s1, r1, 0)
        return carry

    def mix_and_send(dy, carry):
        mix_rows(dy, carry)
        return send_rows(dy, carry)

    mix_and_send(jnp.int32(0), 0)
    halo_forward()
    lax.fori_loop(1, Y, mix_and_send, 0)

    first, second, third = out >> 6, (out >> 2) & 15, out & 3
    t2[...] = (src == second * 16 + third * 4 + first).astype(F32).astype(BF16)
    out, src = out[:128, :128], src[:128, :128]
    first, second, third = out >> 5, (out >> 2) & 7, out & 3
    t3[...] = (src == second * 16 + third * 4 + first).astype(F32).astype(BF16)
    cotp[:, 0:EDGE, :] = jnp.zeros((ROWS + 2, EDGE, SIZE), BF16)
    cotp[:, EDGE + SIZE :, :] = jnp.zeros((ROWS + 2, EDGE, SIZE), BF16)
    for i in range(3):
        kf[3 * i : 3 * i + 3, :] = kern[i].astype(F32)
    taps[...] = jnp.zeros_like(taps)

    loads[2].wait()
    halo_got()

    @pl.when(me == 0)
    def _():
        cotp[0, EDGE : EDGE + SIZE, :] = jnp.zeros((SIZE, SIZE), BF16)

    @pl.when(me == N - 1)
    def _():
        cotp[ROWS + 1, EDGE : EDGE + SIZE, :] = jnp.zeros((SIZE, SIZE), BF16)

    parts = SIZE // STEP

    def tile(it):
        r = it // (parts * parts)
        at = aligned(lax.rem(it // parts, parts) * STEP, STEP)
        lanes = pl.ds(aligned(lax.rem(it, parts) * STEP, STEP), STEP)
        wide = pl.ds(at, STEP + 2 * EDGE)
        return r, pl.ds(at, STEP), wide, lanes

    inner = slice(EDGE, EDGE + STEP)
    span = STEP + 2 * EDGE

    def shifted(x):
        return (pltpu.roll(x, span - 1, 0)[inner], x[inner], pltpu.roll(x, 1, 0)[inner])

    def conv(it, carry):
        r, cols, wide, lanes = tile(it)
        rows = [cotp[r + 2 - i, wide, lanes].astype(F32) for i in range(3)]
        sums = []
        for j in range(3):
            term = rows[0] * kf[j : j + 1, lanes]
            for i in (1, 2):
                term = term + rows[i] * kf[3 * i + j : 3 * i + j + 1, lanes]
            sums.append(term)
        grad = (
            pltpu.roll(sums[0], span - 1, 0)[inner]
            + sums[1][inner]
            + pltpu.roll(sums[2], 1, 0)[inner]
        )
        gate = jax.nn.sigmoid(tok[r, cols, lanes].astype(F32))
        grad = grad * gate
        mid[r, cols, lanes] = grad.astype(BF16)
        hold[r, cols, lanes] = grad * (1.0 - gate)
        return carry

    lax.fori_loop(0, ROWS * parts * parts, conv, 0)

    def send_grad(dy, carry):
        band, cols = band_of(dy)
        pack(band, [mid[q, cols, :] for q in range(ROWS)], s2)
        send(dy, s2, r2, 1)
        return carry

    lax.fori_loop(0, Y, send_grad, 0)

    loads[3].wait()
    wait_got(r1, 0)
    unpack(r1, xs)
    wait_sent(s1, 0)

    def mix_columns(dy, carry):
        band, cols = band_of(dy)
        pack(band, [dot(cf[q, cols, :], xs[q]).astype(BF16) for q in range(ROWS)], s1)
        send(dy, s1, r3, 2)
        return carry

    lax.fori_loop(0, Y, mix_columns, 0)

    wait_got(r2, 1)
    unpack(r2, gs)
    wait_sent(s2, 1)

    def back_columns(dy, carry):
        band, cols = band_of(dy)
        pack(
            band,
            [dot(cf[q, :, cols], gs[q], ((0,), (0,))).astype(BF16) for q in range(ROWS)],
            s2,
        )
        return carry

    def group(i):
        dy = lax.rem(i, 2) * 2 + lax.div(lax.rem(i, 4), 2)
        late = 2 + lax.rem(1 + i + lax.div(i, 4), 2)
        return dy, jnp.where(i < 8, lax.div(i, 4), late)

    def send_back(i, carry):
        dy, pair = group(i)

        @pl.when(i == 0)
        def _():
            send_self(s2, r4, last_sem.at[0])

        for which in range(2):
            send_z(dy, offset(pair, which), s2, r4, 3, last_sem.at[i])
        return carry

    lax.fori_loop(0, Y, back_columns, 0)
    lax.fori_loop(0, 8, send_back, 0)

    def half_of(which):
        return pl.ds(aligned(which * (SIZE // 2), SIZE // 2), SIZE // 2)

    def column_copy(q):
        return pltpu.make_async_remote_copy(
            src_ref=col_out.at[q],
            dst_ref=col_got.at[q],
            send_sem=col_send.at[q],
            recv_sem=col_recv.at[q],
            device_id=other,
            device_id_type=MESH,
        )

    def column_away(q, carry):
        col_out[q] = dot(gs[q, half_of(1 - h), :], xs[q], ((1,), (1,))).astype(BF16)
        column_copy(q).start()
        return carry

    lax.fori_loop(0, ROWS, column_away, 0)

    wait_got(r3, 2)
    unpack(r3, mid)

    def gated(it, carry):
        r, cols, wide, lanes = tile(it)
        mixed = mid[r, cols, lanes].astype(F32)
        gate = jax.nn.sigmoid(tok[r, cols, lanes].astype(F32))
        cells = (mixed * gate).astype(BF16).astype(F32)
        hold[r, cols, lanes] = hold[r, cols, lanes] * mixed
        for i in range(3):
            row = cotp[r + 2 - i, wide, lanes].astype(F32)
            for j, moved in enumerate(shifted(row)):
                term = (cells * moved).reshape(STEP // 8, 8, STEP)
                taps[3 * i + j, :, lanes] += jnp.sum(term, axis=0)
        return carry

    lax.fori_loop(0, ROWS * parts * parts, gated, 0)

    steps = (
        (Z, 0, lambda i: (y, lax.rem(z + i, Z) * XC + xc, h)),
        (Y, Z - 1, lambda i: (lax.rem(y + i, Y), tk, h)),
        (XC, Z + Y - 2, lambda i: (y, z * XC + lax.rem(xc + i, XC), h)),
    )

    def sum_start(k):
        size, slot, peer = steps[k]
        for i in range(1, size):
            pltpu.make_async_remote_copy(
                src_ref=total.at[k],
                dst_ref=held.at[slot + i - 1],
                send_sem=sum_send.at[k],
                recv_sem=sum_recv.at[k],
                device_id=peer(i),
                device_id_type=MESH,
            ).start()

    def sum_finish(k):
        size, slot, _ = steps[k]
        part = held.at[pl.ds(slot, size - 1)]
        pltpu.make_async_copy(part, part, sum_recv.at[k]).wait()
        total[k + 1] = total[k] + jnp.sum(held[slot : slot + size - 1], axis=0)

    def sum_sent(k):
        size, slot, _ = steps[k]
        part = held.at[pl.ds(slot, size - 1)]
        pltpu.make_async_copy(part, part, sum_send.at[k]).wait()

    total[0] = jnp.zeros((16, SIZE), F32)
    for k in range(9):
        total[0, k : k + 1, :] = jnp.sum(taps[k], axis=0, keepdims=True)
    sum_start(0)
    lax.fori_loop(8, 16, send_back, 0)

    def column_store(q):
        return pltpu.make_async_copy(col_done.at[q], gcol_h.at[q], store_sem.at[q])

    def column_here(q, carry):
        term = dot(gs[q, half_of(h), :], xs[q], ((1,), (1,)))
        column_copy(q).wait_recv()
        col_done[q] = (term + col_got[q].astype(F32)).astype(BF16)
        column_store(q).start()
        return carry

    def source(dy):
        band = lax.rem(y + Y - dy, Y)
        cols = pl.ds(aligned(band * BAND, BAND), BAND)
        return band, cols, band // 2 != h, aligned(lax.rem(band, 2) * BAND, BAND)

    def row_copy(at):
        part = pl.ds(at, 16)
        return pltpu.make_async_remote_copy(
            src_ref=row_out.at[:, part, :],
            dst_ref=row_got.at[:, part, :],
            send_sem=row_send.at[at // BAND],
            recv_sem=row_recv.at[at // BAND],
            device_id=other,
            device_id_type=MESH,
        )

    def row_store(slot):
        part = pl.ds(slot * BAND, BAND)
        return pltpu.make_async_copy(
            row_done.at[:, part, :], grow_h.at[:, part, :], store_sem.at[ROWS + slot]
        )

    def row_here(dy):
        band, cols, away, base = source(dy)

        @pl.when(jnp.logical_not(away))
        def _():
            part = pl.ds(base, BAND)
            got = row_got.at[:, part, :]
            terms = [dot(grows[q, cols, :], tok[q], ((1,), (1,))) for q in range(ROWS)]
            pltpu.make_async_copy(got, got, row_recv.at[base // BAND]).wait()
            for q in range(ROWS):
                row_done[q, part, :] = (terms[q] + row_got[q, part, :].astype(F32)).astype(BF16)
            row_store(base // BAND).start()

    def arrive(i):
        dy = i % 2 * 2 + i % 4 // 2
        pair = i // 4 if i < 8 else 2 + (1 + i + i // 4) % 2
        band, cols, away, base = source(dy)
        part = r4.at[pl.ds(0, 128), :]
        pltpu.make_async_copy(part, part, last_sem.at[i]).wait()
        zs = [lax.rem(z + Z - dz, Z) for dz in ((0, 4), (2, 6), (3, 5), (1, 7))[pair]]
        blocks = [r4[pl.ds(aligned((band * Z + zz) * 64, 64), 64), :] for zz in zs]
        block = dot(t3[...], jnp.concatenate(blocks, axis=0)).astype(BF16)
        for q in range(ROWS):
            for m, zz in enumerate(zs):
                low = 32 * q + 16 * m
                grows[q, pl.ds(aligned(band * BAND + zz * 16, 16), 16), :] = block[low : low + 16]

        @pl.when(away)
        def _():
            for q in range(ROWS):
                term = dot(block[32 * q : 32 * q + 32], tok[q], ((1,), (1,))).astype(BF16)
                for m, zz in enumerate(zs):
                    at = aligned(base + zz * 16, 16)
                    row_out[q, pl.ds(at, 16), :] = term[16 * m : 16 * m + 16]
            for zz in zs:
                row_copy(aligned(base + zz * 16, 16)).start()

    def back(par, q):
        zp = lax.rem(z + par, 2)
        parts = [
            pl.ds(aligned(band * BAND + (zp + 2 * m) * 16, 16), 16)
            for band in range(Y)
            for m in range(Z // 2)
        ]
        factor = jnp.concatenate([rf[q, part, :] for part in parts], axis=0)
        grads = jnp.concatenate([grows[q, part, :] for part in parts], axis=0)
        return hold[q] + dot(factor, grads, ((0,), (0,)))

    def token_store(q):
        return pltpu.make_async_copy(mid.at[q], gtok_h.at[q], store_sem.at[ROWS + 2 + q])

    for i in range(16):
        arrive(i)
        if i == 3:
            lax.fori_loop(0, ROWS, column_here, 0)
        if i == 7:
            for q in range(ROWS):
                hold[q] = back(0, q)
        if i == 8:
            sum_finish(0)
            sum_start(1)
        if i == 12:
            sum_finish(1)
            sum_start(2)
    for q in range(ROWS):
        mid[q] = back(1, q).astype(BF16)
        token_store(q).start()
    sum_finish(2)
    for i in range(3):
        gkern[i] = total[3, 3 * i : 3 * i + 3, :]
    for dy in range(Y):
        row_here(dy)

    wait_sent(s1, 2)
    wait_sent(s2, 3)
    halo_sent()
    for k in range(3):
        sum_sent(k)
    for slot in range(2):
        part = row_out.at[:, pl.ds(slot * BAND, BAND), :]
        pltpu.make_async_copy(part, part, row_send.at[slot]).wait()
        row_store(slot).wait()
    for q in range(ROWS):
        column_copy(q).wait_send()
        column_store(q).wait()
        token_store(q).wait()


def shards(tokens, row_factor, column_factor, kernel, cotangent):
    full = (ROWS, SIZE, SIZE)
    half = (ROWS, SIZE // 2, SIZE)
    flat = (N * CELL, SIZE)
    vmem, dma = pltpu.VMEM, pltpu.SemaphoreType.DMA
    whole = pl.BlockSpec(memory_space=pl.ANY)
    local = pl.BlockSpec(memory_space=pltpu.VMEM)
    return pl.pallas_call(
        mixer,
        out_shape=[
            jax.ShapeDtypeStruct(full, BF16),
            jax.ShapeDtypeStruct(half, BF16),
            jax.ShapeDtypeStruct(half, BF16),
            jax.ShapeDtypeStruct((3, 3, SIZE), F32),
        ],
        in_specs=[whole, whole, whole, local, whole],
        out_specs=[whole, whole, whole, local],
        scratch_shapes=[
            vmem(full, BF16), vmem(full, BF16), vmem(full, BF16),
            vmem((ROWS + 2, SIZE + 2 * EDGE, SIZE), BF16),
            vmem(flat, BF16), vmem(flat, BF16),
            vmem(flat, BF16), vmem(flat, BF16), vmem(flat, BF16), vmem(flat, BF16),
            vmem(full, BF16), vmem(full, BF16), vmem(full, F32), vmem(full, BF16), vmem(full, BF16),
            vmem(half, BF16), vmem(half, BF16), vmem(half, BF16), vmem(half, BF16),
            vmem(half, BF16), vmem(half, BF16),
            vmem((2, SIZE // XC, SIZE), BF16), vmem((9, 8, SIZE), F32), vmem((16, SIZE), F32),
            vmem((4, 16, SIZE), F32), vmem((Z + Y + XC - 3, 16, SIZE), F32),
            vmem((256, 256), BF16), vmem((256, 256), BF16), vmem((128, 128), BF16),
            dma((4,)), dma((2,)), dma((2,)), dma((2,)), dma((2,)), dma((2,)), dma((4,)), dma((3,)), dma((4 * Y,)),
            dma((ROWS,)), dma((ROWS,)), dma((2,)), dma((2,)), dma((3,)), dma((3,)),
            dma((2 * ROWS + 2,)),
        ],
        name="mixer",
        compiler_params=pltpu.CompilerParams(
            collective_id=1, has_side_effects=True, vmem_limit_bytes=49 * 2**20
        ),
        cost_estimate=pl.CostEstimate(
            flops=7 * 10**9, bytes_accessed=12 * 2**20, transcendentals=4 * 10**6
        ),
    )(tokens, row_factor, column_factor, kernel, cotangent)


def solution(mesh):
    return jax.shard_map(
        lambda *args: tuple(shards(*args)),
        mesh=mesh,
        in_specs=(
            P(("grp", "tok"), None, "ch"),
            P(("grp", "tok"), None, None),
            P(("grp", "tok"), None, None),
            P(None, None, "ch"),
            P(("grp", "tok"), None, "ch"),
        ),
        out_specs=(
            P(("grp", "tok"), None, "ch"),
            P(("grp", "tok"), "ch", None),
            P(("grp", "tok"), "ch", None),
            P(None, None, "ch"),
        ),
        check_vma=False,
    )
```

```python
import jax
import jax.numpy as jnp
from jax import lax
from jax.experimental import pallas as pl
from jax.experimental.pallas import tpu as pltpu
from jax.sharding import PartitionSpec as P

MESH = pl.DeviceIdType.MESH
F32, BF16 = jnp.float32, jnp.bfloat16
Y, Z, XC = 4, 8, 4
N = Y * Z * XC
ROWS = 4
SIZE = 512
CELL = ROWS * ROWS
BAND = SIZE // Y
EDGE = 16
STEP = 128


def dot(a, b, contract=((1,), (0,))):
    return lax.dot_general(a, b, (contract, ((), ())), preferred_element_type=F32)


def aligned(value, multiple):
    return pl.multiple_of(value, multiple)


def mixer(
    tok_h, rf_h, cf_h, kern, cot_h,
    gtok_h, grow_h, gcol_h, gkern,
    tok, rf, cf, cotp, s1, s2, r1, r2, r3, r4, xs, gs, hold, mid, grows,
    row_out, col_out, row_got, col_got, row_done, col_done, relay, taps, kf, total, held, t1, t2, t3,
    load_sem, halo_send, halo_recv, hand_send, hand_recv, pass_send, send_sem, recv_sem, last_sem,
    col_send, col_recv, row_send, row_recv, sum_send, sum_recv, store_sem,
):
    y, tk, h = lax.axis_index("grp"), lax.axis_index("tok"), lax.axis_index("ch")
    z, xc = tk // XC, lax.rem(tk, XC)
    me = y * (Z * XC) + tk
    other = (y, tk, 1 - h)

    def device(t):
        return (lax.div(t, Z * XC), lax.rem(t, Z * XC), h)

    loads = [
        pltpu.make_async_copy(tok_h, tok, load_sem.at[0]),
        pltpu.make_async_copy(rf_h, rf, load_sem.at[1]),
        pltpu.make_async_copy(cot_h, cotp.at[pl.ds(1, ROWS), pl.ds(EDGE, SIZE), :], load_sem.at[2]),
        pltpu.make_async_copy(cf_h, cf, load_sem.at[3]),
    ]
    for load in loads[:2]:
        load.start()

    barrier = pltpu.get_barrier_semaphore()

    for dy in range(Y):
        band = lax.rem(y + dy, Y)

        def greet(i, carry):
            to = (band, lax.rem(tk + i, Z * XC), h)
            pl.semaphore_signal(barrier, inc=1, device_id=to, device_id_type=MESH)
            return carry

        lax.fori_loop(1 if dy == 0 else 0, Z * XC, greet, 0)
    pl.semaphore_signal(barrier, inc=1, device_id=other, device_id_type=MESH)

    out = lax.broadcasted_iota(jnp.int32, (256, 256), 0)
    src = lax.broadcasted_iota(jnp.int32, (256, 256), 1)
    first, second, third = out >> 4, (out >> 2) & 3, out & 3
    t1[...] = (src == second * 64 + first * 4 + third).astype(F32).astype(BF16)
    quarter = SIZE // XC
    first_of_z = y * (Z * XC) + z * XC
    up, down = lax.rem(me + N - 1, N), lax.rem(me + 1, N)
    up_z, down_z = lax.rem(first_of_z + N - 1, N), lax.rem(first_of_z + XC, N)
    ways = (
        (0, ROWS - 1, 0, XC - 1, down, down_z),
        (1, 0, ROWS + 1, 0, up, up_z),
    )

    def halo_copy(way, source, cols, sem, to):
        return pltpu.make_async_remote_copy(
            src_ref=source,
            dst_ref=cotp.at[ways[way][2], cols, :],
            send_sem=sem,
            recv_sem=halo_recv.at[way],
            device_id=device(to),
            device_id_type=MESH,
        )

    def halo_whole(way):
        _, row, _, _, to, _ = ways[way]
        return halo_copy(way, cot_h.at[row], pl.ds(EDGE, SIZE), halo_send.at[way], to)

    def halo_own(way):
        _, row, _, end, to, _ = ways[way]
        source = cot_h.at[row, pl.ds(end * quarter, quarter), :]
        return halo_copy(way, source, pl.ds(EDGE + end * quarter, quarter), halo_send.at[way], to)

    def halo_hand(way, k):
        row = ways[way][1]
        return pltpu.make_async_remote_copy(
            src_ref=cot_h.at[row, pl.ds(k * quarter, quarter), :],
            dst_ref=relay.at[way],
            send_sem=hand_send.at[way],
            recv_sem=hand_recv.at[way],
            device_id=(y, z * XC + k, h),
            device_id_type=MESH,
        )

    def halo_pass(way):
        cols = pl.ds(aligned(EDGE + xc * quarter, EDGE), quarter)
        return halo_copy(way, relay.at[way], cols, pass_send.at[way], ways[way][5])

    def halo_start():
        for way, _, _, end, _, _ in ways:

            @pl.when(xc == end)
            def _():
                for k in range(XC):
                    if k != end:
                        halo_hand(way, k).start()
                halo_own(way).start()

    def halo_forward():
        for way, _, _, end, _, _ in ways:

            @pl.when(xc != end)
            def _():
                pltpu.make_async_copy(relay.at[way], relay.at[way], hand_recv.at[way]).wait()
                halo_pass(way).start()
                halo_whole(way).start()

    def halo_got():
        for way, _, row, _, _, _ in ways:
            part = cotp.at[row, pl.ds(EDGE, SIZE), :]
            pltpu.make_async_copy(part, part, halo_recv.at[way]).wait()

    def halo_sent():
        for way, _, _, end, _, _ in ways:

            @pl.when(xc == end)
            def _():
                part = cotp.at[0, pl.ds(EDGE, (XC - 1) * quarter), :]
                pltpu.make_async_copy(part, part, hand_send.at[way]).wait()
                halo_own(way).wait_send()

            @pl.when(xc != end)
            def _():
                halo_whole(way).wait_send()
                halo_pass(way).wait_send()

    def pack(band, parts, buf):
        for half in range(2):
            stack = jnp.concatenate([p[64 * half : 64 * half + 64] for p in parts], axis=0)
            at = aligned(band * (Z * XC * CELL) + half * 256, 256)
            buf[pl.ds(at, 256), :] = dot(t1[...], stack).astype(BF16)

    def offset(pair, which):
        first = jnp.where(pair == 0, 0, jnp.where(pair == 1, 2, jnp.where(pair == 2, 3, 1)))
        second = jnp.where(pair == 0, 4, jnp.where(pair == 1, 6, jnp.where(pair == 2, 5, 7)))
        return jnp.where(which == 0, first, second)

    def send_self(buf, dst, sem):
        part = pl.ds(aligned(me * CELL, CELL), CELL)
        pltpu.make_async_copy(buf.at[part, :], dst.at[part, :], sem).start()

    def send_z(dy, dz, buf, dst, k, sem):
        band, to_z = lax.rem(y + dy, Y), lax.rem(z + dz, Z)
        for i in range(XC):
            to = to_z * XC + lax.rem(xc + i, XC)

            def go():
                at = aligned((band * (Z * XC) + to) * CELL, CELL)
                pltpu.make_async_remote_copy(
                    src_ref=buf.at[pl.ds(at, CELL), :],
                    dst_ref=dst.at[pl.ds(aligned(me * CELL, CELL), CELL), :],
                    send_sem=send_sem.at[k],
                    recv_sem=sem,
                    device_id=(band, to, h),
                    device_id_type=MESH,
                ).start()

            if i == 0:
                pl.when(jnp.logical_or(dy > 0, dz > 0))(go)
            else:
                go()

    def send(dy, buf, dst, k):
        @pl.when(dy == 0)
        def _():
            send_self(buf, dst, recv_sem.at[k])

        def one(n, carry):
            dz = offset(lax.div(n, 2), lax.rem(n, 2))
            send_z(dy, dz, buf, dst, k, recv_sem.at[k])
            return carry

        lax.fori_loop(0, Z, one, 0)

    def wait_sent(buf, k):
        part = buf.at[pl.ds(0, (N - 1) * CELL), :]
        pltpu.make_async_copy(part, part, send_sem.at[k]).wait()

    def wait_got(buf, k):
        pltpu.make_async_copy(buf, buf, recv_sem.at[k]).wait()

    def unpack(buf, dst):
        def one(b, carry):
            block = dot(t2[...], buf[pl.ds(aligned(b * 256, 256), 256), :]).astype(BF16)
            for w in range(ROWS):
                dst[w, pl.ds(aligned(b * 64, 64), 64), :] = block[64 * w : 64 * w + 64]
            return carry

        lax.fori_loop(0, N * CELL // 256, one, 0)

    def band_of(dy):
        band = lax.rem(y + dy, Y)
        return band, pl.ds(aligned(band * BAND, BAND), BAND)

    pl.semaphore_wait(barrier, N)
    halo_start()

    loads[0].wait()
    loads[1].wait()
    for load in loads[2:]:
        load.start()

    def mix_rows(dy, carry):
        band, cols = band_of(dy)
        pack(band, [dot(rf[q, cols, :], tok[q]).astype(BF16) for q in range(ROWS)], s1)
        return carry

    def send_rows(dy, carry):
        send(dy, s1, r1, 0)
        return carry

    def mix_and_send(dy, carry):
        mix_rows(dy, carry)
        return send_rows(dy, carry)

    mix_and_send(jnp.int32(0), 0)
    halo_forward()
    lax.fori_loop(1, Y, mix_and_send, 0)

    first, second, third = out >> 6, (out >> 2) & 15, out & 3
    t2[...] = (src == second * 16 + third * 4 + first).astype(F32).astype(BF16)
    out, src = out[:128, :128], src[:128, :128]
    first, second, third = out >> 5, (out >> 2) & 7, out & 3
    t3[...] = (src == second * 16 + third * 4 + first).astype(F32).astype(BF16)
    cotp[:, 0:EDGE, :] = jnp.zeros((ROWS + 2, EDGE, SIZE), BF16)
    cotp[:, EDGE + SIZE :, :] = jnp.zeros((ROWS + 2, EDGE, SIZE), BF16)
    for i in range(3):
        kf[3 * i : 3 * i + 3, :] = kern[i].astype(F32)
    taps[...] = jnp.zeros_like(taps)

    loads[2].wait()
    halo_got()

    @pl.when(me == 0)
    def _():
        cotp[0, EDGE : EDGE + SIZE, :] = jnp.zeros((SIZE, SIZE), BF16)

    @pl.when(me == N - 1)
    def _():
        cotp[ROWS + 1, EDGE : EDGE + SIZE, :] = jnp.zeros((SIZE, SIZE), BF16)

    parts = SIZE // STEP

    def tile(it):
        r = it // (parts * parts)
        at = aligned(lax.rem(it // parts, parts) * STEP, STEP)
        lanes = pl.ds(aligned(lax.rem(it, parts) * STEP, STEP), STEP)
        wide = pl.ds(at, STEP + 2 * EDGE)
        return r, pl.ds(at, STEP), wide, lanes

    inner = slice(EDGE, EDGE + STEP)
    span = STEP + 2 * EDGE

    def shifted(x):
        return (pltpu.roll(x, span - 1, 0)[inner], x[inner], pltpu.roll(x, 1, 0)[inner])

    def conv(it, carry):
        r, cols, wide, lanes = tile(it)
        rows = [cotp[r + 2 - i, wide, lanes].astype(F32) for i in range(3)]
        sums = []
        for j in range(3):
            term = rows[0] * kf[j : j + 1, lanes]
            for i in (1, 2):
                term = term + rows[i] * kf[3 * i + j : 3 * i + j + 1, lanes]
            sums.append(term)
        grad = (
            pltpu.roll(sums[0], span - 1, 0)[inner]
            + sums[1][inner]
            + pltpu.roll(sums[2], 1, 0)[inner]
        )
        gate = jax.nn.sigmoid(tok[r, cols, lanes].astype(F32))
        grad = grad * gate
        mid[r, cols, lanes] = grad.astype(BF16)
        hold[r, cols, lanes] = grad * (1.0 - gate)
        return carry

    lax.fori_loop(0, ROWS * parts * parts, conv, 0)

    def send_grad(dy, carry):
        band, cols = band_of(dy)
        pack(band, [mid[q, cols, :] for q in range(ROWS)], s2)
        send(dy, s2, r2, 1)
        return carry

    lax.fori_loop(0, Y, send_grad, 0)

    loads[3].wait()
    wait_got(r1, 0)
    unpack(r1, xs)
    wait_sent(s1, 0)

    def mix_columns(dy, carry):
        band, cols = band_of(dy)
        pack(band, [dot(cf[q, cols, :], xs[q]).astype(BF16) for q in range(ROWS)], s1)
        send(dy, s1, r3, 2)
        return carry

    lax.fori_loop(0, Y, mix_columns, 0)

    wait_got(r2, 1)
    unpack(r2, gs)
    wait_sent(s2, 1)

    def back_columns(dy, carry):
        band, cols = band_of(dy)
        pack(
            band,
            [dot(cf[q, :, cols], gs[q], ((0,), (0,))).astype(BF16) for q in range(ROWS)],
            s2,
        )
        return carry

    def group(i):
        dy = lax.rem(i, 2) * 2 + lax.div(lax.rem(i, 4), 2)
        late = 2 + lax.rem(1 + i + lax.div(i, 4), 2)
        return dy, jnp.where(i < 8, lax.div(i, 4), late)

    def send_back(i, carry):
        dy, pair = group(i)

        @pl.when(i == 0)
        def _():
            send_self(s2, r4, last_sem.at[0])

        for which in range(2):
            send_z(dy, offset(pair, which), s2, r4, 3, last_sem.at[i])
        return carry

    lax.fori_loop(0, Y, back_columns, 0)
    lax.fori_loop(0, 8, send_back, 0)

    def half_of(which):
        return pl.ds(aligned(which * (SIZE // 2), SIZE // 2), SIZE // 2)

    def column_copy(q):
        return pltpu.make_async_remote_copy(
            src_ref=col_out.at[q],
            dst_ref=col_got.at[q],
            send_sem=col_send.at[q],
            recv_sem=col_recv.at[q],
            device_id=other,
            device_id_type=MESH,
        )

    def column_away(q, carry):
        col_out[q] = dot(gs[q, half_of(1 - h), :], xs[q], ((1,), (1,))).astype(BF16)
        column_copy(q).start()
        return carry

    lax.fori_loop(0, ROWS, column_away, 0)

    wait_got(r3, 2)
    unpack(r3, mid)

    def gated(it, carry):
        r, cols, wide, lanes = tile(it)
        mixed = mid[r, cols, lanes].astype(F32)
        gate = jax.nn.sigmoid(tok[r, cols, lanes].astype(F32))
        cells = (mixed * gate).astype(BF16).astype(F32)
        hold[r, cols, lanes] = hold[r, cols, lanes] * mixed
        for i in range(3):
            row = cotp[r + 2 - i, wide, lanes].astype(F32)
            for j, moved in enumerate(shifted(row)):
                term = (cells * moved).reshape(STEP // 8, 8, STEP)
                taps[3 * i + j, :, lanes] += jnp.sum(term, axis=0)
        return carry

    lax.fori_loop(0, ROWS * parts * parts, gated, 0)

    steps = (
        (Z, 0, lambda i: (y, lax.rem(z + i, Z) * XC + xc, h)),
        (Y, Z - 1, lambda i: (lax.rem(y + i, Y), tk, h)),
        (XC, Z + Y - 2, lambda i: (y, z * XC + lax.rem(xc + i, XC), h)),
    )

    def sum_start(k):
        size, slot, peer = steps[k]
        for i in range(1, size):
            pltpu.make_async_remote_copy(
                src_ref=total.at[k],
                dst_ref=held.at[slot + i - 1],
                send_sem=sum_send.at[k],
                recv_sem=sum_recv.at[k],
                device_id=peer(i),
                device_id_type=MESH,
            ).start()

    def sum_finish(k):
        size, slot, _ = steps[k]
        part = held.at[pl.ds(slot, size - 1)]
        pltpu.make_async_copy(part, part, sum_recv.at[k]).wait()
        total[k + 1] = total[k] + jnp.sum(held[slot : slot + size - 1], axis=0)

    def sum_sent(k):
        size, slot, _ = steps[k]
        part = held.at[pl.ds(slot, size - 1)]
        pltpu.make_async_copy(part, part, sum_send.at[k]).wait()

    total[0] = jnp.zeros((16, SIZE), F32)
    for k in range(9):
        total[0, k : k + 1, :] = jnp.sum(taps[k], axis=0, keepdims=True)
    sum_start(0)
    lax.fori_loop(8, 16, send_back, 0)

    def column_store(q):
        return pltpu.make_async_copy(col_done.at[q], gcol_h.at[q], store_sem.at[q])

    def column_here(q, carry):
        term = dot(gs[q, half_of(h), :], xs[q], ((1,), (1,)))
        column_copy(q).wait_recv()
        col_done[q] = (term + col_got[q].astype(F32)).astype(BF16)
        column_store(q).start()
        return carry

    def source(dy):
        band = lax.rem(y + Y - dy, Y)
        cols = pl.ds(aligned(band * BAND, BAND), BAND)
        return band, cols, band // 2 != h, aligned(lax.rem(band, 2) * BAND, BAND)

    def row_copy(at):
        part = pl.ds(at, 16)
        return pltpu.make_async_remote_copy(
            src_ref=row_out.at[:, part, :],
            dst_ref=row_got.at[:, part, :],
            send_sem=row_send.at[at // BAND],
            recv_sem=row_recv.at[at // BAND],
            device_id=other,
            device_id_type=MESH,
        )

    def row_store(slot):
        part = pl.ds(slot * BAND, BAND)
        return pltpu.make_async_copy(
            row_done.at[:, part, :], grow_h.at[:, part, :], store_sem.at[ROWS + slot]
        )

    def row_here(dy):
        band, cols, away, base = source(dy)

        @pl.when(jnp.logical_not(away))
        def _():
            part = pl.ds(base, BAND)
            got = row_got.at[:, part, :]
            terms = [dot(grows[q, cols, :], tok[q], ((1,), (1,))) for q in range(ROWS)]
            pltpu.make_async_copy(got, got, row_recv.at[base // BAND]).wait()
            for q in range(ROWS):
                row_done[q, part, :] = (terms[q] + row_got[q, part, :].astype(F32)).astype(BF16)
            row_store(base // BAND).start()

    def arrive(i):
        dy = i % 2 * 2 + i % 4 // 2
        pair = i // 4 if i < 8 else 2 + (1 + i + i // 4) % 2
        band, cols, away, base = source(dy)
        part = r4.at[pl.ds(0, 128), :]
        pltpu.make_async_copy(part, part, last_sem.at[i]).wait()
        zs = [lax.rem(z + Z - dz, Z) for dz in ((0, 4), (2, 6), (3, 5), (1, 7))[pair]]
        blocks = [r4[pl.ds(aligned((band * Z + zz) * 64, 64), 64), :] for zz in zs]
        block = dot(t3[...], jnp.concatenate(blocks, axis=0)).astype(BF16)
        for q in range(ROWS):
            for m, zz in enumerate(zs):
                low = 32 * q + 16 * m
                grows[q, pl.ds(aligned(band * BAND + zz * 16, 16), 16), :] = block[low : low + 16]

        @pl.when(away)
        def _():
            for q in range(ROWS):
                term = dot(block[32 * q : 32 * q + 32], tok[q], ((1,), (1,))).astype(BF16)
                for m, zz in enumerate(zs):
                    at = aligned(base + zz * 16, 16)
                    row_out[q, pl.ds(at, 16), :] = term[16 * m : 16 * m + 16]
            for zz in zs:
                row_copy(aligned(base + zz * 16, 16)).start()

    def back(par, q):
        zp = lax.rem(z + par, 2)
        parts = [
            pl.ds(aligned(band * BAND + (zp + 2 * m) * 16, 16), 16)
            for band in range(Y)
            for m in range(Z // 2)
        ]
        factor = jnp.concatenate([rf[q, part, :] for part in parts], axis=0)
        grads = jnp.concatenate([grows[q, part, :] for part in parts], axis=0)
        return hold[q] + dot(factor, grads, ((0,), (0,)))

    def token_store(q):
        return pltpu.make_async_copy(mid.at[q], gtok_h.at[q], store_sem.at[ROWS + 2 + q])

    for i in range(16):
        arrive(i)
        if i == 3:
            lax.fori_loop(0, ROWS, column_here, 0)
        if i == 7:
            for q in range(ROWS):
                hold[q] = back(0, q)
        if i == 8:
            sum_finish(0)
            sum_start(1)
        if i == 12:
            sum_finish(1)
            sum_start(2)
    for q in range(ROWS):
        mid[q] = back(1, q).astype(BF16)
        token_store(q).start()
    sum_finish(2)
    for i in range(3):
        gkern[i] = total[3, 3 * i : 3 * i + 3, :]
    for dy in range(Y):
        row_here(dy)

    wait_sent(s1, 2)
    wait_sent(s2, 3)
    halo_sent()
    for k in range(3):
        sum_sent(k)
    for slot in range(2):
        part = row_out.at[:, pl.ds(slot * BAND, BAND), :]
        pltpu.make_async_copy(part, part, row_send.at[slot]).wait()
        row_store(slot).wait()
    for q in range(ROWS):
        column_copy(q).wait_send()
        column_store(q).wait()
        token_store(q).wait()


def hand_out(tok_v, row_v, col_v, kern_v, tok_h, row_h, col_h, kern_h, sems):
    pairs = ((tok_v, tok_h), (row_v, row_h), (col_v, col_h), (kern_v, kern_h))
    copies = [pltpu.make_async_copy(a, b, sems.at[i]) for i, (a, b) in enumerate(pairs)]
    for copy in copies:
        copy.start()
    for copy in copies:
        copy.wait()


def shards(tokens, row_factor, column_factor, kernel, cotangent):
    whole = pl.BlockSpec(memory_space=pl.ANY)
    results = compute(tokens, row_factor, column_factor, kernel, cotangent)
    return pl.pallas_call(
        hand_out,
        out_shape=[jax.ShapeDtypeStruct(r.shape, r.dtype) for r in results],
        in_specs=[whole] * 4,
        out_specs=[whole] * 4,
        scratch_shapes=[pltpu.SemaphoreType.DMA((4,))],
        name="hand_out",
        compiler_params=pltpu.CompilerParams(vmem_limit_bytes=2**20),
    )(*results)


def compute(tokens, row_factor, column_factor, kernel, cotangent):
    full = (ROWS, SIZE, SIZE)
    half = (ROWS, SIZE // 2, SIZE)
    flat = (N * CELL, SIZE)
    vmem, dma = pltpu.VMEM, pltpu.SemaphoreType.DMA
    whole = pl.BlockSpec(memory_space=pl.ANY)
    local = pl.BlockSpec(memory_space=pltpu.VMEM)
    return pl.pallas_call(
        mixer,
        out_shape=[
            jax.ShapeDtypeStruct(full, BF16),
            jax.ShapeDtypeStruct(half, BF16),
            jax.ShapeDtypeStruct(half, BF16),
            jax.ShapeDtypeStruct((3, 3, SIZE), F32),
        ],
        in_specs=[whole, whole, whole, local, whole],
        out_specs=[whole, whole, whole, local],
        scratch_shapes=[
            vmem(full, BF16), vmem(full, BF16), vmem(full, BF16),
            vmem((ROWS + 2, SIZE + 2 * EDGE, SIZE), BF16),
            vmem(flat, BF16), vmem(flat, BF16),
            vmem(flat, BF16), vmem(flat, BF16), vmem(flat, BF16), vmem(flat, BF16),
            vmem(full, BF16), vmem(full, BF16), vmem(full, F32), vmem(full, BF16), vmem(full, BF16),
            vmem(half, BF16), vmem(half, BF16), vmem(half, BF16), vmem(half, BF16),
            vmem(half, BF16), vmem(half, BF16),
            vmem((2, SIZE // XC, SIZE), BF16), vmem((9, 8, SIZE), F32), vmem((16, SIZE), F32),
            vmem((4, 16, SIZE), F32), vmem((Z + Y + XC - 3, 16, SIZE), F32),
            vmem((256, 256), BF16), vmem((256, 256), BF16), vmem((128, 128), BF16),
            dma((4,)), dma((2,)), dma((2,)), dma((2,)), dma((2,)), dma((2,)), dma((4,)), dma((3,)), dma((4 * Y,)),
            dma((ROWS,)), dma((ROWS,)), dma((2,)), dma((2,)), dma((3,)), dma((3,)),
            dma((2 * ROWS + 2,)),
        ],
        name="mixer",
        compiler_params=pltpu.CompilerParams(
            collective_id=1, has_side_effects=True, vmem_limit_bytes=49 * 2**20
        ),
        cost_estimate=pl.CostEstimate(
            flops=7 * 10**9, bytes_accessed=12 * 2**20, transcendentals=4 * 10**6
        ),
    )(tokens, row_factor, column_factor, kernel, cotangent)


def solution(mesh):
    return jax.shard_map(
        lambda *args: tuple(shards(*args)),
        mesh=mesh,
        in_specs=(
            P(("grp", "tok"), None, "ch"),
            P(("grp", "tok"), None, None),
            P(("grp", "tok"), None, None),
            P(None, None, "ch"),
            P(("grp", "tok"), None, "ch"),
        ),
        out_specs=(
            P(("grp", "tok"), None, "ch"),
            P(("grp", "tok"), "ch", None),
            P(("grp", "tok"), "ch", None),
            P(None, None, "ch"),
        ),
        check_vma=False,
    )
```

```python
import jax
import jax.numpy as jnp
from jax import lax
from jax.experimental import pallas as pl
from jax.experimental.pallas import tpu as pltpu
from jax.sharding import PartitionSpec as P

MESH = pl.DeviceIdType.MESH
F32, BF16 = jnp.float32, jnp.bfloat16
Y, Z, XC = 4, 8, 4
N = Y * Z * XC
ROWS = 4
SIZE = 512
CELL = ROWS * ROWS
BAND = SIZE // Y
EDGE = 16
STEP = 128


def dot(a, b, contract=((1,), (0,))):
    return lax.dot_general(a, b, (contract, ((), ())), preferred_element_type=F32)


def aligned(value, multiple):
    return pl.multiple_of(value, multiple)


def mixer(
    tok_h, rf_h, cf_h, kern, cot_h,
    gtok_h, grow_h, gcol_h, gkern,
    tok, rf, cf, cotp, s1, s2, r1, r2, r3, r4, xs, gs, hold, mid, grows,
    row_out, col_out, row_got, col_got, row_done, col_done, relay, taps, kf, total, held, t1, t2, t3,
    load_sem, halo_send, halo_recv, hand_send, hand_recv, pass_send, send_sem, recv_sem, last_sem,
    col_send, col_recv, row_send, row_recv, sum_send, sum_recv, store_sem,
):
    y, tk, h = lax.axis_index("grp"), lax.axis_index("tok"), lax.axis_index("ch")
    z, xc = tk // XC, lax.rem(tk, XC)
    me = y * (Z * XC) + tk
    other = (y, tk, 1 - h)

    def device(t):
        return (lax.div(t, Z * XC), lax.rem(t, Z * XC), h)

    loads = [
        pltpu.make_async_copy(tok_h, tok, load_sem.at[0]),
        pltpu.make_async_copy(rf_h, rf, load_sem.at[1]),
        pltpu.make_async_copy(cot_h, cotp.at[pl.ds(1, ROWS), pl.ds(EDGE, SIZE), :], load_sem.at[2]),
        pltpu.make_async_copy(cf_h, cf, load_sem.at[3]),
    ]
    for load in loads[:2]:
        load.start()

    barrier = pltpu.get_barrier_semaphore()

    for dy in range(Y):
        band = lax.rem(y + dy, Y)

        def greet(i, carry):
            for k in range(XC):
                to = (band, i * XC + k, h)
                if dy == 0:

                    @pl.when(i * XC + k != tk)
                    def _():
                        pl.semaphore_signal(barrier, inc=1, device_id=to, device_id_type=MESH)

                else:
                    pl.semaphore_signal(barrier, inc=1, device_id=to, device_id_type=MESH)
            return carry

        lax.fori_loop(0, Z, greet, 0)
    pl.semaphore_signal(barrier, inc=1, device_id=other, device_id_type=MESH)

    out = lax.broadcasted_iota(jnp.int32, (256, 256), 0)
    src = lax.broadcasted_iota(jnp.int32, (256, 256), 1)
    first, second, third = out >> 4, (out >> 2) & 3, out & 3
    t1[...] = (src == second * 64 + first * 4 + third).astype(F32).astype(BF16)
    quarter = SIZE // XC
    first_of_z = y * (Z * XC) + z * XC
    up, down = lax.rem(me + N - 1, N), lax.rem(me + 1, N)
    up_z, down_z = lax.rem(first_of_z + N - 1, N), lax.rem(first_of_z + XC, N)
    ways = (
        (0, ROWS - 1, 0, XC - 1, down, down_z),
        (1, 0, ROWS + 1, 0, up, up_z),
    )

    def halo_copy(way, source, cols, sem, to):
        return pltpu.make_async_remote_copy(
            src_ref=source,
            dst_ref=cotp.at[ways[way][2], cols, :],
            send_sem=sem,
            recv_sem=halo_recv.at[way],
            device_id=device(to),
            device_id_type=MESH,
        )

    def halo_whole(way):
        _, row, _, _, to, _ = ways[way]
        return halo_copy(way, cot_h.at[row], pl.ds(EDGE, SIZE), halo_send.at[way], to)

    def halo_own(way):
        _, row, _, end, to, _ = ways[way]
        source = cot_h.at[row, pl.ds(end * quarter, quarter), :]
        return halo_copy(way, source, pl.ds(EDGE + end * quarter, quarter), halo_send.at[way], to)

    def halo_hand(way, k):
        row = ways[way][1]
        return pltpu.make_async_remote_copy(
            src_ref=cot_h.at[row, pl.ds(k * quarter, quarter), :],
            dst_ref=relay.at[way],
            send_sem=hand_send.at[way],
            recv_sem=hand_recv.at[way],
            device_id=(y, z * XC + k, h),
            device_id_type=MESH,
        )

    def halo_pass(way):
        cols = pl.ds(aligned(EDGE + xc * quarter, EDGE), quarter)
        return halo_copy(way, relay.at[way], cols, pass_send.at[way], ways[way][5])

    def halo_start():
        for way, _, _, end, _, _ in ways:

            @pl.when(xc == end)
            def _():
                for k in range(XC):
                    if k != end:
                        halo_hand(way, k).start()
                halo_own(way).start()

    def halo_forward():
        for way, _, _, end, _, _ in ways:

            @pl.when(xc != end)
            def _():
                pltpu.make_async_copy(relay.at[way], relay.at[way], hand_recv.at[way]).wait()
                halo_pass(way).start()
                halo_whole(way).start()

    def halo_got():
        for way, _, row, _, _, _ in ways:
            part = cotp.at[row, pl.ds(EDGE, SIZE), :]
            pltpu.make_async_copy(part, part, halo_recv.at[way]).wait()

    def halo_sent():
        for way, _, _, end, _, _ in ways:

            @pl.when(xc == end)
            def _():
                part = cotp.at[0, pl.ds(EDGE, (XC - 1) * quarter), :]
                pltpu.make_async_copy(part, part, hand_send.at[way]).wait()
                halo_own(way).wait_send()

            @pl.when(xc != end)
            def _():
                halo_whole(way).wait_send()
                halo_pass(way).wait_send()

    def pack(band, parts, buf):
        for half in range(2):
            stack = jnp.concatenate([p[64 * half : 64 * half + 64] for p in parts], axis=0)
            at = aligned(band * (Z * XC * CELL) + half * 256, 256)
            buf[pl.ds(at, 256), :] = dot(t1[...], stack).astype(BF16)

    def offset(pair, which):
        first = jnp.where(pair == 0, 0, jnp.where(pair == 1, 2, jnp.where(pair == 2, 3, 1)))
        second = jnp.where(pair == 0, 4, jnp.where(pair == 1, 6, jnp.where(pair == 2, 5, 7)))
        return jnp.where(which == 0, first, second)

    def send_self(buf, dst, sem):
        part = pl.ds(aligned(me * CELL, CELL), CELL)
        pltpu.make_async_copy(buf.at[part, :], dst.at[part, :], sem).start()

    def send_z(dy, dz, buf, dst, k, sem):
        band, to_z = lax.rem(y + dy, Y), lax.rem(z + dz, Z)
        for i in range(XC):
            to = to_z * XC + lax.rem(xc + i, XC)

            def go():
                at = aligned((band * (Z * XC) + to) * CELL, CELL)
                pltpu.make_async_remote_copy(
                    src_ref=buf.at[pl.ds(at, CELL), :],
                    dst_ref=dst.at[pl.ds(aligned(me * CELL, CELL), CELL), :],
                    send_sem=send_sem.at[k],
                    recv_sem=sem,
                    device_id=(band, to, h),
                    device_id_type=MESH,
                ).start()

            if i == 0:
                pl.when(jnp.logical_or(dy > 0, dz > 0))(go)
            else:
                go()

    def send(dy, buf, dst, k):
        @pl.when(dy == 0)
        def _():
            send_self(buf, dst, recv_sem.at[k])

        def one(n, carry):
            dz = offset(lax.div(n, 2), lax.rem(n, 2))
            send_z(dy, dz, buf, dst, k, recv_sem.at[k])
            return carry

        lax.fori_loop(0, Z, one, 0)

    def wait_sent(buf, k):
        part = buf.at[pl.ds(0, (N - 1) * CELL), :]
        pltpu.make_async_copy(part, part, send_sem.at[k]).wait()

    def wait_got(buf, k):
        pltpu.make_async_copy(buf, buf, recv_sem.at[k]).wait()

    def unpack(buf, dst):
        def one(b, carry):
            block = dot(t2[...], buf[pl.ds(aligned(b * 256, 256), 256), :]).astype(BF16)
            for w in range(ROWS):
                dst[w, pl.ds(aligned(b * 64, 64), 64), :] = block[64 * w : 64 * w + 64]
            return carry

        lax.fori_loop(0, N * CELL // 256, one, 0)

    def band_of(dy):
        band = lax.rem(y + dy, Y)
        return band, pl.ds(aligned(band * BAND, BAND), BAND)

    pl.semaphore_wait(barrier, N)
    halo_start()

    loads[0].wait()
    loads[1].wait()
    for load in loads[2:]:
        load.start()

    def mix_rows(dy, carry):
        band, cols = band_of(dy)
        pack(band, [dot(rf[q, cols, :], tok[q]).astype(BF16) for q in range(ROWS)], s1)
        return carry

    def send_rows(dy, carry):
        send(dy, s1, r1, 0)
        return carry

    def mix_and_send(dy, carry):
        mix_rows(dy, carry)
        return send_rows(dy, carry)

    mix_and_send(jnp.int32(0), 0)
    halo_forward()
    lax.fori_loop(1, Y, mix_and_send, 0)

    first, second, third = out >> 6, (out >> 2) & 15, out & 3
    t2[...] = (src == second * 16 + third * 4 + first).astype(F32).astype(BF16)
    out, src = out[:128, :128], src[:128, :128]
    first, second, third = out >> 5, (out >> 2) & 7, out & 3
    t3[...] = (src == second * 16 + third * 4 + first).astype(F32).astype(BF16)
    cotp[:, 0:EDGE, :] = jnp.zeros((ROWS + 2, EDGE, SIZE), BF16)
    cotp[:, EDGE + SIZE :, :] = jnp.zeros((ROWS + 2, EDGE, SIZE), BF16)
    for i in range(3):
        kf[3 * i : 3 * i + 3, :] = kern[i].astype(F32)
    taps[...] = jnp.zeros_like(taps)

    loads[2].wait()
    halo_got()

    @pl.when(me == 0)
    def _():
        cotp[0, EDGE : EDGE + SIZE, :] = jnp.zeros((SIZE, SIZE), BF16)

    @pl.when(me == N - 1)
    def _():
        cotp[ROWS + 1, EDGE : EDGE + SIZE, :] = jnp.zeros((SIZE, SIZE), BF16)

    parts = SIZE // STEP

    def tile(it):
        r = it // (parts * parts)
        at = aligned(lax.rem(it // parts, parts) * STEP, STEP)
        lanes = pl.ds(aligned(lax.rem(it, parts) * STEP, STEP), STEP)
        wide = pl.ds(at, STEP + 2 * EDGE)
        return r, pl.ds(at, STEP), wide, lanes

    inner = slice(EDGE, EDGE + STEP)
    span = STEP + 2 * EDGE

    def shifted(x):
        return (pltpu.roll(x, span - 1, 0)[inner], x[inner], pltpu.roll(x, 1, 0)[inner])

    def conv(it, carry):
        r, cols, wide, lanes = tile(it)
        rows = [cotp[r + 2 - i, wide, lanes].astype(F32) for i in range(3)]
        sums = []
        for j in range(3):
            term = rows[0] * kf[j : j + 1, lanes]
            for i in (1, 2):
                term = term + rows[i] * kf[3 * i + j : 3 * i + j + 1, lanes]
            sums.append(term)
        grad = (
            pltpu.roll(sums[0], span - 1, 0)[inner]
            + sums[1][inner]
            + pltpu.roll(sums[2], 1, 0)[inner]
        )
        gate = jax.nn.sigmoid(tok[r, cols, lanes].astype(F32))
        grad = grad * gate
        mid[r, cols, lanes] = grad.astype(BF16)
        hold[r, cols, lanes] = grad * (1.0 - gate)
        return carry

    lax.fori_loop(0, ROWS * parts * parts, conv, 0)

    def send_grad(dy, carry):
        band, cols = band_of(dy)
        pack(band, [mid[q, cols, :] for q in range(ROWS)], s2)
        send(dy, s2, r2, 1)
        return carry

    lax.fori_loop(0, Y, send_grad, 0)

    loads[3].wait()
    wait_got(r1, 0)
    unpack(r1, xs)
    wait_sent(s1, 0)

    def mix_columns(dy, carry):
        band, cols = band_of(dy)
        pack(band, [dot(cf[q, cols, :], xs[q]).astype(BF16) for q in range(ROWS)], s1)
        send(dy, s1, r3, 2)
        return carry

    lax.fori_loop(0, Y, mix_columns, 0)

    wait_got(r2, 1)
    unpack(r2, gs)
    wait_sent(s2, 1)

    def back_columns(dy, carry):
        band, cols = band_of(dy)
        pack(
            band,
            [dot(cf[q, :, cols], gs[q], ((0,), (0,))).astype(BF16) for q in range(ROWS)],
            s2,
        )
        return carry

    def group(i):
        dy = lax.rem(i, 2) * 2 + lax.div(lax.rem(i, 4), 2)
        late = 2 + lax.rem(1 + i + lax.div(i, 4), 2)
        return dy, jnp.where(i < 8, lax.div(i, 4), late)

    def send_back(i, carry):
        dy, pair = group(i)

        @pl.when(i == 0)
        def _():
            send_self(s2, r4, last_sem.at[0])

        for which in range(2):
            send_z(dy, offset(pair, which), s2, r4, 3, last_sem.at[i])
        return carry

    lax.fori_loop(0, Y, back_columns, 0)
    lax.fori_loop(0, 8, send_back, 0)

    def half_of(which):
        return pl.ds(aligned(which * (SIZE // 2), SIZE // 2), SIZE // 2)

    def column_copy(q):
        return pltpu.make_async_remote_copy(
            src_ref=col_out.at[q],
            dst_ref=col_got.at[q],
            send_sem=col_send.at[q],
            recv_sem=col_recv.at[q],
            device_id=other,
            device_id_type=MESH,
        )

    def column_away(q, carry):
        col_out[q] = dot(gs[q, half_of(1 - h), :], xs[q], ((1,), (1,))).astype(BF16)
        column_copy(q).start()
        return carry

    lax.fori_loop(0, ROWS, column_away, 0)

    wait_got(r3, 2)
    unpack(r3, mid)

    def gated(it, carry):
        r, cols, wide, lanes = tile(it)
        mixed = mid[r, cols, lanes].astype(F32)
        gate = jax.nn.sigmoid(tok[r, cols, lanes].astype(F32))
        cells = (mixed * gate).astype(BF16).astype(F32)
        hold[r, cols, lanes] = hold[r, cols, lanes] * mixed
        for i in range(3):
            row = cotp[r + 2 - i, wide, lanes].astype(F32)
            for j, moved in enumerate(shifted(row)):
                term = (cells * moved).reshape(STEP // 8, 8, STEP)
                taps[3 * i + j, :, lanes] += jnp.sum(term, axis=0)
        return carry

    lax.fori_loop(0, ROWS * parts * parts, gated, 0)

    steps = (
        (Z, 0, lambda i: (y, lax.rem(z + i, Z) * XC + xc, h)),
        (Y, Z - 1, lambda i: (lax.rem(y + i, Y), tk, h)),
        (XC, Z + Y - 2, lambda i: (y, z * XC + lax.rem(xc + i, XC), h)),
    )

    def sum_start(k):
        size, slot, peer = steps[k]
        for i in range(1, size):
            pltpu.make_async_remote_copy(
                src_ref=total.at[k],
                dst_ref=held.at[slot + i - 1],
                send_sem=sum_send.at[k],
                recv_sem=sum_recv.at[k],
                device_id=peer(i),
                device_id_type=MESH,
            ).start()

    def sum_finish(k):
        size, slot, _ = steps[k]
        part = held.at[pl.ds(slot, size - 1)]
        pltpu.make_async_copy(part, part, sum_recv.at[k]).wait()
        total[k + 1] = total[k] + jnp.sum(held[slot : slot + size - 1], axis=0)

    def sum_sent(k):
        size, slot, _ = steps[k]
        part = held.at[pl.ds(slot, size - 1)]
        pltpu.make_async_copy(part, part, sum_send.at[k]).wait()

    total[0] = jnp.zeros((16, SIZE), F32)
    for k in range(9):
        total[0, k : k + 1, :] = jnp.sum(taps[k], axis=0, keepdims=True)
    sum_start(0)
    lax.fori_loop(8, 16, send_back, 0)

    def column_store(q):
        return pltpu.make_async_copy(col_done.at[q], gcol_h.at[q], store_sem.at[q])

    def column_here(q, carry):
        term = dot(gs[q, half_of(h), :], xs[q], ((1,), (1,)))
        column_copy(q).wait_recv()
        col_done[q] = (term + col_got[q].astype(F32)).astype(BF16)
        column_store(q).start()
        return carry

    def source(dy):
        band = lax.rem(y + Y - dy, Y)
        cols = pl.ds(aligned(band * BAND, BAND), BAND)
        return band, cols, band // 2 != h, aligned(lax.rem(band, 2) * BAND, BAND)

    def row_copy(at):
        part = pl.ds(at, 16)
        return pltpu.make_async_remote_copy(
            src_ref=row_out.at[:, part, :],
            dst_ref=row_got.at[:, part, :],
            send_sem=row_send.at[at // BAND],
            recv_sem=row_recv.at[at // BAND],
            device_id=other,
            device_id_type=MESH,
        )

    def row_store(slot):
        part = pl.ds(slot * BAND, BAND)
        return pltpu.make_async_copy(
            row_done.at[:, part, :], grow_h.at[:, part, :], store_sem.at[ROWS + slot]
        )

    def row_here(dy):
        band, cols, away, base = source(dy)

        @pl.when(jnp.logical_not(away))
        def _():
            part = pl.ds(base, BAND)
            got = row_got.at[:, part, :]
            terms = [dot(grows[q, cols, :], tok[q], ((1,), (1,))) for q in range(ROWS)]
            pltpu.make_async_copy(got, got, row_recv.at[base // BAND]).wait()
            for q in range(ROWS):
                row_done[q, part, :] = (terms[q] + row_got[q, part, :].astype(F32)).astype(BF16)
            row_store(base // BAND).start()

    def arrive(i):
        dy = i % 2 * 2 + i % 4 // 2
        pair = i // 4 if i < 8 else 2 + (1 + i + i // 4) % 2
        band, cols, away, base = source(dy)
        part = r4.at[pl.ds(0, 128), :]
        pltpu.make_async_copy(part, part, last_sem.at[i]).wait()
        zs = [lax.rem(z + Z - dz, Z) for dz in ((0, 4), (2, 6), (3, 5), (1, 7))[pair]]
        blocks = [r4[pl.ds(aligned((band * Z + zz) * 64, 64), 64), :] for zz in zs]
        block = dot(t3[...], jnp.concatenate(blocks, axis=0)).astype(BF16)
        for q in range(ROWS):
            for m, zz in enumerate(zs):
                low = 32 * q + 16 * m
                grows[q, pl.ds(aligned(band * BAND + zz * 16, 16), 16), :] = block[low : low + 16]

        @pl.when(away)
        def _():
            for q in range(ROWS):
                term = dot(block[32 * q : 32 * q + 32], tok[q], ((1,), (1,))).astype(BF16)
                for m, zz in enumerate(zs):
                    at = aligned(base + zz * 16, 16)
                    row_out[q, pl.ds(at, 16), :] = term[16 * m : 16 * m + 16]
            for zz in zs:
                row_copy(aligned(base + zz * 16, 16)).start()

    def back(par, q):
        zp = lax.rem(z + par, 2)
        parts = [
            pl.ds(aligned(band * BAND + (zp + 2 * m) * 16, 16), 16)
            for band in range(Y)
            for m in range(Z // 2)
        ]
        factor = jnp.concatenate([rf[q, part, :] for part in parts], axis=0)
        grads = jnp.concatenate([grows[q, part, :] for part in parts], axis=0)
        return hold[q] + dot(factor, grads, ((0,), (0,)))

    def token_store(q):
        return pltpu.make_async_copy(mid.at[q], gtok_h.at[q], store_sem.at[ROWS + 2 + q])

    for i in range(16):
        arrive(i)
        if i == 3:
            lax.fori_loop(0, ROWS, column_here, 0)
        if i == 7:
            for q in range(ROWS):
                hold[q] = back(0, q)
        if i == 8:
            sum_finish(0)
            sum_start(1)
        if i == 12:
            sum_finish(1)
            sum_start(2)
    for q in range(ROWS):
        mid[q] = back(1, q).astype(BF16)
        token_store(q).start()
    sum_finish(2)
    for i in range(3):
        gkern[i] = total[3, 3 * i : 3 * i + 3, :]
    for dy in (0, 2, 1, 3):
        row_here(dy)

    wait_sent(s1, 2)
    wait_sent(s2, 3)
    halo_sent()
    for k in range(3):
        sum_sent(k)
    for slot in range(2):
        part = row_out.at[:, pl.ds(slot * BAND, BAND), :]
        pltpu.make_async_copy(part, part, row_send.at[slot]).wait()
        row_store(slot).wait()
    for q in range(ROWS):
        column_copy(q).wait_send()
        column_store(q).wait()
        token_store(q).wait()


def hand_out(tok_v, row_v, col_v, kern_v, tok_h, row_h, col_h, kern_h, sems):
    pairs = ((tok_v, tok_h), (row_v, row_h), (col_v, col_h), (kern_v, kern_h))
    copies = [pltpu.make_async_copy(a, b, sems.at[i]) for i, (a, b) in enumerate(pairs)]
    for copy in copies:
        copy.start()
    for copy in copies:
        copy.wait()


def shards(tokens, row_factor, column_factor, kernel, cotangent):
    whole = pl.BlockSpec(memory_space=pl.ANY)
    results = compute(tokens, row_factor, column_factor, kernel, cotangent)
    return pl.pallas_call(
        hand_out,
        out_shape=[jax.ShapeDtypeStruct(r.shape, r.dtype) for r in results],
        in_specs=[whole] * 4,
        out_specs=[whole] * 4,
        scratch_shapes=[pltpu.SemaphoreType.DMA((4,))],
        name="hand_out",
        compiler_params=pltpu.CompilerParams(vmem_limit_bytes=2**20),
    )(*results)


def compute(tokens, row_factor, column_factor, kernel, cotangent):
    full = (ROWS, SIZE, SIZE)
    half = (ROWS, SIZE // 2, SIZE)
    flat = (N * CELL, SIZE)
    vmem, dma = pltpu.VMEM, pltpu.SemaphoreType.DMA
    whole = pl.BlockSpec(memory_space=pl.ANY)
    local = pl.BlockSpec(memory_space=pltpu.VMEM)
    return pl.pallas_call(
        mixer,
        out_shape=[
            jax.ShapeDtypeStruct(full, BF16),
            jax.ShapeDtypeStruct(half, BF16),
            jax.ShapeDtypeStruct(half, BF16),
            jax.ShapeDtypeStruct((3, 3, SIZE), F32),
        ],
        in_specs=[whole, whole, whole, local, whole],
        out_specs=[whole, whole, whole, local],
        scratch_shapes=[
            vmem(full, BF16), vmem(full, BF16), vmem(full, BF16),
            vmem((ROWS + 2, SIZE + 2 * EDGE, SIZE), BF16),
            vmem(flat, BF16), vmem(flat, BF16),
            vmem(flat, BF16), vmem(flat, BF16), vmem(flat, BF16), vmem(flat, BF16),
            vmem(full, BF16), vmem(full, BF16), vmem(full, F32), vmem(full, BF16), vmem(full, BF16),
            vmem(half, BF16), vmem(half, BF16), vmem(half, BF16), vmem(half, BF16),
            vmem(half, BF16), vmem(half, BF16),
            vmem((2, SIZE // XC, SIZE), BF16), vmem((9, 8, SIZE), F32), vmem((16, SIZE), F32),
            vmem((4, 16, SIZE), F32), vmem((Z + Y + XC - 3, 16, SIZE), F32),
            vmem((256, 256), BF16), vmem((256, 256), BF16), vmem((128, 128), BF16),
            dma((4,)), dma((2,)), dma((2,)), dma((2,)), dma((2,)), dma((2,)), dma((4,)), dma((3,)), dma((4 * Y,)),
            dma((ROWS,)), dma((ROWS,)), dma((2,)), dma((2,)), dma((3,)), dma((3,)),
            dma((2 * ROWS + 2,)),
        ],
        name="mixer",
        compiler_params=pltpu.CompilerParams(
            collective_id=1, has_side_effects=True, vmem_limit_bytes=49 * 2**20
        ),
        cost_estimate=pl.CostEstimate(
            flops=7 * 10**9, bytes_accessed=12 * 2**20, transcendentals=4 * 10**6
        ),
    )(tokens, row_factor, column_factor, kernel, cotangent)


def solution(mesh):
    return jax.shard_map(
        lambda *args: tuple(shards(*args)),
        mesh=mesh,
        in_specs=(
            P(("grp", "tok"), None, "ch"),
            P(("grp", "tok"), None, None),
            P(("grp", "tok"), None, None),
            P(None, None, "ch"),
            P(("grp", "tok"), None, "ch"),
        ),
        out_specs=(
            P(("grp", "tok"), None, "ch"),
            P(("grp", "tok"), "ch", None),
            P(("grp", "tok"), "ch", None),
            P(None, None, "ch"),
        ),
        check_vma=False,
    )
```
